32 devices in a mesh: grp: 8 (over y, x, core), loc: 4 (over z).
Axes of the slice: x: 2, y: 2, z: 4, core: 2. Of those that a mesh axis runs over, the one named last changes fastest.
Arguments:
- tokens: bfloat16 [4096, 2048], P(('grp', 'loc')), may hold values from -6 to 6
- norm_gain: bfloat16 [2048], replicated, may hold values from 0.099609375 to 1.8984375
- w_gate: bfloat16 [32, 2048, 384], P(('grp', 'loc')), may hold values from -0.125 to 0.125
- w_up: bfloat16 [32, 2048, 384], P(('grp', 'loc')), may hold values from -0.125 to 0.125
- w_down: bfloat16 [32, 384, 2048], P(('grp', 'loc')), may hold values from -0.21875 to 0.21875
- expert_ids: int32 [4096, 8], P(('grp', 'loc')), may hold values from 0 to 15, as said below
- gate_num: int32 [4096, 8], P(('grp', 'loc')), may hold values from 32 to 255
Outputs:
- mixed: bfloat16 [4096, 2048], P(('grp', 'loc'))
The draws below stay inside these ranges and needn't reach their ends.
Inputs may be any that keep to these rules, and one draw needn't show every extreme that they name: `expert_ids`: each token names 4 different groups (group of expert e: e // 2) and two different experts in each, listed group after group in increasing order. Of the 128 tokens of one device at most 128 use any one group, and every device has a group used by exactly 128 of its tokens. The tokens of all devices with one loc index use each group exactly 512 times in all, and each expert of that group exactly 512 times.
All inputs are finite; a program needn't handle non-finite values.
Results may differ from the reference program's by a relative error of at most 0.0038.
Values may be sent and summed in bfloat16 or wider, within the bound.
A program may use at most 128 MiB of HBM per device.

```python
import jax
import jax.numpy as jnp
from jax import lax

D = 2048
FF = 768
TOPK = 8
GTOP = 4
TOK_DEV = 128
TOKENS = 4096
EXPERTS = 16
N_GRP = 8
N_LOC = 4


def draw_expert_ids(key, part):
    average = TOK_DEV * GTOP // N_GRP
    recv_total = TOK_DEV * GTOP
    per_group = N_LOC // 2
    key_base, key_token, key_recv = jax.random.split(key, 3)

    def base_counts(subkey):
        key_order, key_amount = jax.random.split(subkey)
        order = jax.random.permutation(key_order, N_GRP)
        amount = jax.random.randint(key_amount, (N_GRP // 2,), 0, average + 1)
        amount = amount.at[0].set(average)
        values = jnp.concatenate([average + amount, average - amount]).astype(jnp.int32)
        return jnp.zeros((N_GRP,), jnp.int32).at[order].set(values)
    base = jax.vmap(base_counts)(jax.random.split(key_base, N_LOC))
    senders = jnp.arange(N_GRP)
    shifted = (senders[None, :] - senders[:, None]) % N_GRP
    counts = jnp.transpose(base[:, shifted], (1, 0, 2))
    run_ends = jnp.cumsum(counts, axis=2)
    entries = jnp.arange(GTOP * TOK_DEV)
    entry_group = jnp.sum((run_ends[:, :, None, :] <= entries[None, None, :, None]).astype(jnp.int32), axis=3)
    token_keys = jax.random.split(key_token, N_GRP * N_LOC)
    token_place = jax.vmap(lambda subkey: jax.random.permutation(subkey, TOK_DEV))(token_keys)
    token_place = token_place.reshape(N_GRP, N_LOC, TOK_DEV)
    columns = jnp.arange(GTOP) * TOK_DEV
    lookup = token_place[:, :, :, None] + columns[None, None, None, :]
    groups = jnp.take_along_axis(entry_group, lookup.reshape(N_GRP, N_LOC, TOK_DEV * GTOP), axis=2)
    groups = groups.reshape(N_GRP, N_LOC, TOK_DEV, GTOP)
    member = jnp.any(groups[..., None] == jnp.arange(N_GRP), axis=3).astype(jnp.int32)
    ranking = jnp.cumsum(member, axis=2) - 1
    starts = jnp.cumsum(counts, axis=0) - counts
    starts_full = jnp.broadcast_to(starts[:, :, None, :], (N_GRP, N_LOC, TOK_DEV, N_GRP))
    position = jnp.take_along_axis(starts_full, groups, axis=3) + jnp.take_along_axis(ranking, groups, axis=3)
    recv_keys = jax.random.split(key_recv, N_GRP * N_LOC)
    recv_perm = jax.vmap(lambda subkey: jax.random.permutation(subkey, recv_total))(recv_keys)
    recv_perm = recv_perm.reshape(N_GRP, N_LOC, recv_total)
    locals_index = jnp.arange(N_LOC)[None, :, None, None]
    mapped = recv_perm[groups, locals_index, position]
    first_local = mapped % per_group
    offset_step = 1 + mapped // per_group % (per_group - 1)
    second_local = (first_local + offset_step) % per_group
    chosen_ids = jnp.stack([groups * per_group + first_local, groups * per_group + second_local], axis=4)
    return chosen_ids.reshape(N_GRP * N_LOC * TOK_DEV, GTOP * 2).astype(jnp.int32)


def place_ends(array, key, least, top_value):
    longest = array.shape.index(max(array.shape))
    spots = []
    for shift in (0, 1):
        where = [jax.random.randint(jax.random.fold_in(key, axis), (), 0, length) for axis, length in enumerate(array.shape)]
        where[longest] = (where[longest] + shift) % array.shape[longest]
        spots.append(tuple(where))
    return array.at[spots[0]].set(least).at[spots[1]].set(top_value)


def block_levels(stream_key, extent, cuts, smallest, largest):
    gain = 1.0
    for dim, shards_of in cuts:
        heights = jax.random.uniform(jax.random.fold_in(jax.random.fold_in(stream_key, 6), dim), (shards_of,), jnp.float32, smallest / len(cuts), largest / len(cuts))
        gain = gain * jnp.repeat(jnp.exp(heights), extent[dim] // shards_of).reshape((-1,) + (1,) * (len(extent) - 1 - dim))
    return gain


def scatter_about(stream_key, extent, width, most, shards=(), dtype=jnp.bfloat16):
    loudness = block_levels(stream_key, extent, shards, -0.22, 0.18) if shards else 1.0
    values = jax.random.normal(stream_key, extent, jnp.float32) * width * loudness
    return jnp.minimum(jnp.maximum(values, -most), most).astype(dtype)


def setup_inputs(seed: int = 0) -> dict:
    key_list = jax.random.split(jax.random.key(seed), 8)
    return {
        "tokens": scatter_about(key_list[0], (TOKENS, D), 1.0, 6.0, ((0, 32),)),
        "norm_gain": jnp.clip(1.0 + 0.18 * jax.random.normal(key_list[1], (D,), jnp.float32), 0.099609375, 1.8984375).astype(jnp.bfloat16),
        "w_gate": scatter_about(key_list[2], (2 * EXPERTS, D, FF // 2), D ** -0.5, 0.125, ((0, 32),)),
        "w_up": scatter_about(key_list[3], (2 * EXPERTS, D, FF // 2), D ** -0.5, 0.125, ((0, 32),)),
        "w_down": scatter_about(key_list[4], (2 * EXPERTS, FF // 2, D), FF ** -0.5, 0.21875, ((0, 32),)),
        "expert_ids": draw_expert_ids(jax.random.fold_in(key_list[7], 71), 0),
        "gate_num": place_ends(jax.random.randint(key_list[6], (TOKENS, TOPK), 32, 256), jax.random.fold_in(key_list[6], 1), 32, 255).astype(jnp.int32),
    }


epsilon = 1e-06
denominator = 1024.0

def expert_out(rows_in, gate_full, up_full, down_full):
    gate_act = jnp.dot(rows_in, gate_full, preferred_element_type=jnp.float32)
    up_act = jnp.dot(rows_in, up_full, preferred_element_type=jnp.float32)
    hidden = (jax.nn.silu(gate_act) * up_act).astype(jnp.bfloat16)
    return jnp.dot(hidden, down_full, preferred_element_type=jnp.float32).astype(jnp.bfloat16)

def reference(tokens, norm_gain, w_gate, w_up, w_down, expert_ids, gate_num):
    per_group = N_LOC // 2
    group_rows = TOKENS * GTOP // N_GRP
    each_expert = TOKENS * TOPK // EXPERTS
    inputs_float = tokens.astype(jnp.float32)
    inv_scale = lax.rsqrt(lax.optimization_barrier(jnp.mean(inputs_float * inputs_float, axis=-1, keepdims=True)) + epsilon)
    normed = (inputs_float * inv_scale * norm_gain.astype(jnp.float32)).astype(jnp.bfloat16)
    gate_values = gate_num.astype(jnp.float32) / denominator
    owner_group = expert_ids // per_group

    def per_group_step(output_sum, group_index):
        touches = jnp.any(owner_group == group_index, axis=1)
        token_index = jnp.nonzero(touches, size=group_rows)[0]
        ids_group = expert_ids[token_index]
        gates_group = gate_values[token_index]
        inputs_group = normed[token_index]
        accumulator = jnp.zeros((group_rows, D), jnp.float32)
        for expert_local in range(per_group):
            expert_index = group_index * per_group + expert_local
            matches = ids_group == expert_index
            weight = lax.optimization_barrier(jnp.sum(jnp.where(matches, gates_group, 0.0), axis=1))
            rows_index = jnp.nonzero(jnp.any(matches, axis=1), size=each_expert)[0]
            gate_full = jnp.concatenate([w_gate[2 * expert_index], w_gate[2 * expert_index + 1]], axis=1)
            up_full = jnp.concatenate([w_up[2 * expert_index], w_up[2 * expert_index + 1]], axis=1)
            down_full = jnp.concatenate([w_down[2 * expert_index], w_down[2 * expert_index + 1]], axis=0)
            outputs = expert_out(inputs_group[rows_index], gate_full, up_full, down_full)
            accumulator = accumulator.at[rows_index].add(weight[rows_index][:, None] * outputs.astype(jnp.float32))
        group_part = lax.optimization_barrier(accumulator.astype(jnp.bfloat16)).astype(jnp.float32)
        return (output_sum.at[token_index].add(group_part), None)
    output_sum, unused = lax.scan(per_group_step, jnp.zeros((TOKENS, D), jnp.float32), jnp.arange(N_GRP))
    return (inputs_float + output_sum).astype(jnp.bfloat16)
```

```python
import jax
import jax.numpy as jnp
from jax import lax
from jax.experimental import pallas as pl
from jax.experimental.pallas import tpu as pltpu
from jax.sharding import PartitionSpec as P

GTOP = 4


epsilon = 1e-06
denominator = 1024.0


def from_partner(value, axis, apart):
    mask = 2**apart
    pairs = [(source, source ^ mask) for source in range(lax.axis_size(axis))]
    return lax.ppermute(value, axis, pairs)


def ordered_pair(own_part, other_part, is_lower, axis_index):
    lower_part = jnp.where(is_lower, own_part, other_part)
    upper_part = jnp.where(is_lower, other_part, own_part)
    return jnp.concatenate([lower_part, upper_part], axis=axis_index)


def routed(tokens, norm_gain, w_gate, w_up, w_down, expert_ids, gate_num):
    group_count = lax.axis_size("grp")
    local_count = lax.axis_size("loc")
    rows_dev, model_width = tokens.shape
    top_count = expert_ids.shape[1]
    experts_group = local_count // 2
    capacity = 2 * rows_dev * GTOP // group_count
    expert_rows = rows_dev * GTOP * (top_count // GTOP) // experts_group
    half_rows = expert_rows // 2
    slots_all = group_count * capacity
    inputs_float = tokens.astype(jnp.float32)
    inv_scale = lax.rsqrt(jnp.mean(inputs_float * inputs_float, axis=-1, keepdims=True) + epsilon)
    normed = (inputs_float * inv_scale * norm_gain.astype(jnp.float32)).astype(jnp.bfloat16)
    owner_group = expert_ids // experts_group
    group_range = jnp.arange(group_count, dtype=jnp.int32)
    member = jnp.any(owner_group[:, :, None] == group_range[None, None, :], axis=1)
    position = jnp.cumsum(member.astype(jnp.int32), axis=0) - 1
    slot_range = jnp.arange(capacity, dtype=jnp.int32)
    slot_table = member.T[:, None, :] & (position.T[:, None, :] == slot_range[None, :, None])
    dispatch_matrix = slot_table.reshape(slots_all, rows_dev).astype(jnp.bfloat16)
    packed = jnp.dot(dispatch_matrix, normed, preferred_element_type=jnp.float32).astype(
        jnp.bfloat16
    )
    packed = packed.reshape(group_count, capacity, model_width)
    filled = jnp.any(slot_table, axis=2).reshape(slots_all)
    token_range = jnp.arange(rows_dev, dtype=jnp.int32)
    source_token = jnp.sum(
        slot_table.astype(jnp.int32) * token_range[None, None, :], axis=2
    ).reshape(slots_all)
    details = jnp.concatenate([expert_ids, gate_num], axis=1)[source_token]
    details = jnp.where(filled[:, None], details, -1).astype(jnp.bfloat16)
    details = details.reshape(group_count, capacity, 2 * top_count)
    arrived, arrived_details = (
        lax.all_to_all(packed, "grp", split_axis=0, concat_axis=0, tiled=True),
        lax.all_to_all(details, "grp", split_axis=0, concat_axis=0, tiled=True),
    )
    arrived = arrived.reshape(slots_all, model_width)
    arrived_details = arrived_details.reshape(slots_all, 2 * top_count).astype(jnp.int32)
    own_group = lax.axis_index("grp")
    own_half = lax.axis_index("loc") % 2
    is_lower = own_half == 0
    arrived_ids = arrived_details[:, :top_count]
    arrived_nums = arrived_details[:, top_count:]
    local_ids = arrived_ids - own_group * experts_group
    inside = (arrived_ids >= 0) & (local_ids >= 0) & (local_ids < experts_group)
    expert_range = jnp.arange(experts_group, dtype=jnp.int32)
    chosen = jnp.any(
        inside[:, :, None] & (local_ids[:, :, None] == expert_range[None, None, :]), axis=1
    )
    ranking = jnp.cumsum(chosen.astype(jnp.int32), axis=0) - 1
    slot_index = jnp.broadcast_to(jnp.arange(slots_all, dtype=jnp.int32)[:, None], chosen.shape)
    base_index = 2 * expert_range[None, :] * expert_rows + ranking
    spill_index = local_count * expert_rows
    target_lower = jnp.where(chosen, base_index, spill_index)
    target_upper = jnp.where(chosen, base_index + expert_rows, spill_index)
    source_slot = jnp.zeros((spill_index,), jnp.int32)
    source_slot = source_slot.at[target_lower.reshape(-1)].set(slot_index.reshape(-1), mode="drop")
    source_slot = source_slot.at[target_upper.reshape(-1)].set(slot_index.reshape(-1), mode="drop")
    outgoing = arrived[source_slot].reshape(local_count, expert_rows, model_width)
    received = lax.all_to_all(outgoing, "loc", split_axis=0, concat_axis=0, tiled=True)
    flat_rows = received.reshape(-1, model_width)
    gate_act = jnp.dot(flat_rows, w_gate[0], preferred_element_type=jnp.float32)
    up_act = jnp.dot(flat_rows, w_up[0], preferred_element_type=jnp.float32)
    hidden = (jax.nn.silu(gate_act) * up_act).astype(jnp.bfloat16)
    hidden = hidden.reshape(local_count, expert_rows, w_gate.shape[2])
    own_hidden = lax.dynamic_slice_in_dim(hidden, own_half * half_rows, half_rows, 1)
    given_hidden = lax.dynamic_slice_in_dim(hidden, (1 - own_half) * half_rows, half_rows, 1)
    taken_hidden, other_down = from_partner((given_hidden, w_down[0]), "loc", 0)
    hidden_full = ordered_pair(own_hidden, taken_hidden, is_lower, 2)
    down_full = ordered_pair(w_down[0], other_down, is_lower, 0)
    result = jnp.dot(
        hidden_full.reshape(-1, hidden_full.shape[2]), down_full, preferred_element_type=jnp.float32
    )
    result = result.astype(jnp.bfloat16).reshape(local_count, half_rows, model_width)
    returned = lax.all_to_all(result, "loc", split_axis=0, concat_axis=0, tiled=True)
    flat_returned = returned.reshape(-1, model_width)
    filled_slot = jnp.any(inside, axis=1)
    first_pick = jnp.argmax(inside, axis=1)
    second_pick = top_count - 1 - jnp.argmax(inside[:, ::-1], axis=1)

    def pick_term(which):
        local_pick = jnp.take_along_axis(local_ids, which[:, None], axis=1)[:, 0]
        local_pick = jnp.where(filled_slot, local_pick, 0)
        rank_pick = jnp.take_along_axis(ranking, local_pick[:, None], axis=1)[:, 0]
        row_pick = (2 * local_pick + rank_pick // half_rows) * half_rows + rank_pick % half_rows
        row_pick = jnp.where(filled_slot, row_pick, 0)
        weight = jnp.take_along_axis(arrived_nums, which[:, None], axis=1)[:, 0]
        weight = jnp.where(filled_slot, weight, 0).astype(jnp.float32) / denominator
        return weight[:, None] * flat_returned[row_pick].astype(jnp.float32)

    group_sum = (pick_term(first_pick) + pick_term(second_pick)).astype(jnp.bfloat16)
    group_sum = group_sum.reshape(group_count, capacity, model_width)
    returned_sums = lax.all_to_all(group_sum, "grp", split_axis=0, concat_axis=0, tiled=True)
    mixed_sum = jnp.dot(
        dispatch_matrix.T,
        returned_sums.reshape(slots_all, model_width),
        preferred_element_type=jnp.float32,
    )
    return (inputs_float + mixed_sum).astype(jnp.bfloat16)


MESH = pl.DeviceIdType.MESH
Z, X, Y, S, FA, FB, R1, R2A, R2B, R3X, R3Y, R4 = 0, 1, 2, 3, 7, 8, 9, 13, 14, 15, 16, 17
KINDS = 18


def flip(value, bit, unit):
    digit = (value // unit) % 2
    return value + unit * ((digit + bit) % 2 - digit)


def fused_kernel(
    tokens_ref, gain_ref, w_gate_ref, w_up_ref, w_down_ref, ids_ref, nums_ref, out_ref,
    rows, sums, from_sibling, diag_in, near_in, z_in, w_in, num_all,
    send_sem, recv_sem, num_send, num_recv,
):
    grp, loc = lax.axis_index("grp"), lax.axis_index("loc")
    n_rows, width = tokens_ref.shape
    half = n_rows // 2
    hidden_units = w_gate_ref.shape[2]
    experts = num_all.shape[1]
    sibling = (flip(grp, 1, 1), loc)
    along_x = (flip(grp, 1, 2), loc)
    along_y = (flip(grp, 1, 4), loc)
    me = grp * 4 + loc
    everyone = 32

    barrier = pltpu.get_barrier_semaphore()

    @pl.loop(1, everyone)
    def _(i):
        other = (me + i) % everyone
        pl.semaphore_signal(barrier, 1, device_id=(other // 4, other % 4), device_id_type=MESH)

    inputs = tokens_ref[...].astype(jnp.float32)
    inv_scale = lax.rsqrt(jnp.mean(inputs * inputs, axis=-1, keepdims=True) + epsilon)
    rows[0, pl.ds(0, n_rows), :] = (
        inputs * inv_scale * gain_ref[...].astype(jnp.float32)
    ).astype(jnp.bfloat16)
    expert_row = lax.broadcasted_iota(jnp.int32, (experts, n_rows), 0)
    numerators = jnp.zeros((experts, n_rows), jnp.int32)
    for k in range(ids_ref.shape[0]):
        numerators += jnp.where(ids_ref[k : k + 1, :] == expert_row, nums_ref[k : k + 1, :], 0)
    num_all[me] = numerators.astype(jnp.float32).astype(jnp.bfloat16)
    pl.semaphore_wait(barrier, everyone - 1)

    def remote(kind, j, source, target, device):
        return pltpu.make_async_remote_copy(
            src_ref=source,
            dst_ref=target,
            send_sem=send_sem.at[kind * 4 + j],
            recv_sem=recv_sem.at[kind * 4 + j],
            device_id=device,
            device_id_type=MESH,
        )

    own, other_core = pl.ds(0, n_rows), pl.ds(n_rows, n_rows)
    first, second = pl.ds(0, half), pl.ds(half, half)

    def partner(j):
        return (grp, flip(flip(loc, j % 2, 1), j // 2, 2))

    def copy_z(j):
        return remote(Z, j, rows.at[0, own], rows.at[4 * j, own], partner(j))

    def copy_x(j):
        return remote(X, j, rows.at[4 * j, own], rows.at[4 * j + 1, own], along_x)

    def copy_y(j):
        return remote(Y, j, rows.at[4 * j, own], rows.at[4 * j + 2, own], along_y)

    def copy_s(j, q):
        t = 4 * j + q
        return remote(S + q, j, rows.at[t, own], rows.at[t, other_core], sibling)

    def copy_fa(j):
        return remote(FA, j, rows.at[4 * j + 1, first], rows.at[4 * j + 3, first], along_y)

    def copy_fb(j):
        return remote(FB, j, rows.at[4 * j + 2, second], rows.at[4 * j + 3, second], along_x)

    def copy_r1(j, q):
        t = 4 * j + q
        return remote(R1 + q, j, rows.at[t, other_core], from_sibling.at[t], sibling)

    def copy_r2a(j):
        return remote(R2A, j, sums.at[4 * j + 3, first], diag_in.at[j, first], along_x)

    def copy_r2b(j):
        return remote(R2B, j, sums.at[4 * j + 3, second], diag_in.at[j, second], along_y)

    def copy_r3x(j):
        return remote(R3X, j, sums.at[4 * j + 1], near_in.at[j, 0], along_x)

    def copy_r3y(j):
        return remote(R3Y, j, sums.at[4 * j + 2], near_in.at[j, 1], along_y)

    def copy_r4(j):
        return remote(R4, j, sums.at[4 * j], z_in.at[j], partner(j))

    def numerator_copy(source, target, device):
        return pltpu.make_async_remote_copy(
            src_ref=source,
            dst_ref=target,
            send_sem=num_send,
            recv_sem=num_recv,
            device_id=device,
            device_id_type=MESH,
        )

    def spread(j):
        copy_x(j).start()
        copy_y(j).start()
        copy_s(j, 0).start()

    def forward(j):
        copy_x(j).wait_recv()
        copy_fa(j).start()
        copy_s(j, 1).start()
        copy_y(j).wait_recv()
        copy_fb(j).start()
        copy_s(j, 2).start()

    def forward_diagonal(j):
        copy_fa(j).wait_recv()
        copy_fb(j).wait_recv()
        copy_s(j, 3).start()

    def add(t, extra=(), place=None):
        place = pl.ds(0, n_rows) if place is None else place
        total = sums[t, place, :].astype(jnp.float32)
        total += from_sibling[t, place, :].astype(jnp.float32)
        for term in extra:
            total += term[place, :].astype(jnp.float32)
        sums[t, place, :] = total.astype(jnp.bfloat16)

    def reduce_diagonal(j):
        copy_r1(j, 3).wait_recv()
        add(4 * j + 3)
        copy_r2a(j).start()
        copy_r2b(j).start()

    def reduce_near(j):
        copy_r1(j, 1).wait_recv()
        add(4 * j + 1, (), first)
        copy_r2b(j).wait_recv()
        add(4 * j + 1, (diag_in.at[j],), second)
        copy_r3x(j).start()
        copy_r1(j, 2).wait_recv()
        add(4 * j + 2, (), second)
        copy_r2a(j).wait_recv()
        add(4 * j + 2, (diag_in.at[j],), first)
        copy_r3y(j).start()

    def reduce_plane(j):
        copy_r1(j, 0).wait_recv()
        copy_r3x(j).wait_recv()
        copy_r3y(j).wait_recv()
        add(4 * j, (near_in.at[j, 0], near_in.at[j, 1]))

    for j in (1, 2, 3):
        copy_z(j).start()
    spread(0)

    @pl.loop(1, everyone)
    def _(i):
        other = (me + i) % everyone
        numerator_copy(num_all.at[me], num_all.at[me], (other // 4, other % 4)).start()

    w_in[:, :hidden_units] = w_gate_ref[0]
    w_in[:, hidden_units:] = w_up_ref[0]
    forward(0)
    copy_z(1).wait_recv()
    spread(1)
    numerator_copy(
        num_all.at[pl.ds(0, everyone - 1)], num_all.at[pl.ds(0, everyone - 1)], sibling
    ).wait_recv()

    own_expert = grp * 2 + loc // 2
    pick = (expert_row == own_expert).astype(jnp.float32).astype(jnp.bfloat16)

    def weights_of(j, q, core_flip):
        source = flip(flip(flip(grp, core_flip, 1), q % 2, 2), q // 2, 4)
        place = source * 4 + partner(j)[1]
        return lax.dot_general(
            num_all[place], pick, (((0,), (0,)), ((), ())), preferred_element_type=jnp.float32
        )[:, :1] * (1.0 / denominator)

    @pl.loop(0, 16)
    def _(t):
        j, q = t // 4, t % 4

        @pl.when(q == 0)
        def _():
            @pl.when(j >= 2)
            def _():
                reduce_plane(j - 2)

                @pl.when(j >= 3)
                def _():
                    copy_r4(j - 2).start()

            copy_s(j, 0).wait_recv()

        @pl.when(q == 1)
        def _():
            @pl.when(j >= 1)
            def _():
                reduce_diagonal(j - 1)

            forward_diagonal(j)
            copy_s(j, 1).wait_recv()

        @pl.when(q == 2)
        def _():
            @pl.when(j >= 1)
            def _():
                reduce_near(j - 1)

            copy_s(j, 2).wait_recv()

        @pl.when(q == 3)
        def _():
            @pl.when(j < 3)
            def _():
                forward(j + 1)

            @pl.when(j < 2)
            def _():
                copy_z(j + 2).wait_recv()
                spread(j + 2)

            copy_s(j, 3).wait_recv()

        both = jnp.dot(rows[t], w_in[...], preferred_element_type=jnp.float32)
        gate_act, up_act = both[:, :hidden_units], both[:, hidden_units:]
        hidden = (jax.nn.silu(gate_act) * up_act).astype(jnp.bfloat16)
        weight = jnp.concatenate([weights_of(j, q, 0), weights_of(j, q, 1)], axis=0)
        step = width // 4
        for part in range(4):
            columns = pl.ds(part * step, step)
            result = jnp.dot(
                hidden, w_down_ref[0, :, columns], preferred_element_type=jnp.float32
            )
            result = (result * weight).astype(jnp.bfloat16)
            sums[t, :, columns] = result[:n_rows]
            rows[t, other_core, columns] = result[n_rows:]
        for which in range(4):
            @pl.when(q == which)
            def _():
                copy_r1(j, which).start()

    reduce_diagonal(3)
    reduce_plane(2)
    copy_r4(2).start()
    reduce_near(3)
    reduce_plane(3)
    copy_r4(3).start()
    total = tokens_ref[...].astype(jnp.float32) + sums[0].astype(jnp.float32)
    for j in (1, 2, 3):
        copy_r4(j).wait_recv()
        total += z_in[j].astype(jnp.float32)
    out_ref[...] = total.astype(jnp.bfloat16)

    @pl.loop(0, 4)
    def _(j):
        @pl.when(j > 0)
        def _():
            copy_z(j).wait_send()
            copy_r4(j).wait_send()

        copy_x(j).wait_send()
        copy_y(j).wait_send()
        for q in range(4):
            copy_s(j, q).wait_send()
            copy_r1(j, q).wait_send()
        for make in (copy_fa, copy_fb, copy_r2a, copy_r2b, copy_r3x, copy_r3y):
            make(j).wait_send()

    numerator_copy(
        num_all.at[pl.ds(0, everyone - 1)], num_all.at[pl.ds(0, everyone - 1)], sibling
    ).wait_send()


def fused(tokens, norm_gain, w_gate, w_up, w_down, expert_ids, gate_num):
    n_rows, width = tokens.shape
    hidden_units = w_gate.shape[2]
    bf16 = jnp.bfloat16
    return pl.pallas_call(
        fused_kernel,
        out_shape=jax.ShapeDtypeStruct(tokens.shape, tokens.dtype),
        in_specs=[pl.BlockSpec(memory_space=pltpu.VMEM)] * 7,
        out_specs=pl.BlockSpec(memory_space=pltpu.VMEM),
        scratch_shapes=[
            pltpu.VMEM((16, 2 * n_rows, width), bf16),
            pltpu.VMEM((16, n_rows, width), bf16),
            pltpu.VMEM((16, n_rows, width), bf16),
            pltpu.VMEM((4, n_rows, width), bf16),
            pltpu.VMEM((4, 2, n_rows, width), bf16),
            pltpu.VMEM((4, n_rows, width), bf16),
            pltpu.VMEM((width, 2 * hidden_units), bf16),
            pltpu.VMEM((32, 16, n_rows), bf16),
            pltpu.SemaphoreType.DMA((KINDS * 4,)),
            pltpu.SemaphoreType.DMA((KINDS * 4,)),
            pltpu.SemaphoreType.DMA,
            pltpu.SemaphoreType.DMA,
        ],
        compiler_params=pltpu.CompilerParams(
            collective_id=0, has_side_effects=True, vmem_limit_bytes=60 * 2**20
        ),
        cost_estimate=pl.CostEstimate(
            flops=2 * 32 * n_rows * width * hidden_units * 3,
            bytes_accessed=2 * width * hidden_units * 3,
            transcendentals=32 * n_rows * hidden_units,
        ),
    )(tokens, norm_gain.reshape(1, width), w_gate, w_up, w_down, expert_ids.T, gate_num.T)


def shards(tokens, *others):
    if (lax.axis_size("grp"), lax.axis_size("loc")) == (8, 4):
        return fused(tokens, *others)
    return routed(tokens, *others)


def solution(mesh):
    return jax.shard_map(
        shards,
        mesh=mesh,
        in_specs=(
            P(("grp", "loc"), None),
            P(),
            P(("grp", "loc"), None, None),
            P(("grp", "loc"), None, None),
            P(("grp", "loc"), None, None),
            P(("grp", "loc"), None),
            P(("grp", "loc"), None),
        ),
        out_specs=P(("grp", "loc"), None),
        check_vma=False,
    )
```

```python
import jax
import jax.numpy as jnp
from jax import lax
from jax.experimental import pallas as pl
from jax.experimental.pallas import tpu as pltpu
from jax.sharding import PartitionSpec as P

GTOP = 4


epsilon = 1e-06
denominator = 1024.0


def from_partner(value, axis, apart):
    mask = 2**apart
    pairs = [(source, source ^ mask) for source in range(lax.axis_size(axis))]
    return lax.ppermute(value, axis, pairs)


def ordered_pair(own_part, other_part, is_lower, axis_index):
    lower_part = jnp.where(is_lower, own_part, other_part)
    upper_part = jnp.where(is_lower, other_part, own_part)
    return jnp.concatenate([lower_part, upper_part], axis=axis_index)


def routed(tokens, norm_gain, w_gate, w_up, w_down, expert_ids, gate_num):
    group_count = lax.axis_size("grp")
    local_count = lax.axis_size("loc")
    rows_dev, model_width = tokens.shape
    top_count = expert_ids.shape[1]
    experts_group = local_count // 2
    capacity = 2 * rows_dev * GTOP // group_count
    expert_rows = rows_dev * GTOP * (top_count // GTOP) // experts_group
    half_rows = expert_rows // 2
    slots_all = group_count * capacity
    inputs_float = tokens.astype(jnp.float32)
    inv_scale = lax.rsqrt(jnp.mean(inputs_float * inputs_float, axis=-1, keepdims=True) + epsilon)
    normed = (inputs_float * inv_scale * norm_gain.astype(jnp.float32)).astype(jnp.bfloat16)
    owner_group = expert_ids // experts_group
    group_range = jnp.arange(group_count, dtype=jnp.int32)
    member = jnp.any(owner_group[:, :, None] == group_range[None, None, :], axis=1)
    position = jnp.cumsum(member.astype(jnp.int32), axis=0) - 1
    slot_range = jnp.arange(capacity, dtype=jnp.int32)
    slot_table = member.T[:, None, :] & (position.T[:, None, :] == slot_range[None, :, None])
    dispatch_matrix = slot_table.reshape(slots_all, rows_dev).astype(jnp.bfloat16)
    packed = jnp.dot(dispatch_matrix, normed, preferred_element_type=jnp.float32).astype(
        jnp.bfloat16
    )
    packed = packed.reshape(group_count, capacity, model_width)
    filled = jnp.any(slot_table, axis=2).reshape(slots_all)
    token_range = jnp.arange(rows_dev, dtype=jnp.int32)
    source_token = jnp.sum(
        slot_table.astype(jnp.int32) * token_range[None, None, :], axis=2
    ).reshape(slots_all)
    details = jnp.concatenate([expert_ids, gate_num], axis=1)[source_token]
    details = jnp.where(filled[:, None], details, -1).astype(jnp.bfloat16)
    details = details.reshape(group_count, capacity, 2 * top_count)
    arrived, arrived_details = (
        lax.all_to_all(packed, "grp", split_axis=0, concat_axis=0, tiled=True),
        lax.all_to_all(details, "grp", split_axis=0, concat_axis=0, tiled=True),
    )
    arrived = arrived.reshape(slots_all, model_width)
    arrived_details = arrived_details.reshape(slots_all, 2 * top_count).astype(jnp.int32)
    own_group = lax.axis_index("grp")
    own_half = lax.axis_index("loc") % 2
    is_lower = own_half == 0
    arrived_ids = arrived_details[:, :top_count]
    arrived_nums = arrived_details[:, top_count:]
    local_ids = arrived_ids - own_group * experts_group
    inside = (arrived_ids >= 0) & (local_ids >= 0) & (local_ids < experts_group)
    expert_range = jnp.arange(experts_group, dtype=jnp.int32)
    chosen = jnp.any(
        inside[:, :, None] & (local_ids[:, :, None] == expert_range[None, None, :]), axis=1
    )
    ranking = jnp.cumsum(chosen.astype(jnp.int32), axis=0) - 1
    slot_index = jnp.broadcast_to(jnp.arange(slots_all, dtype=jnp.int32)[:, None], chosen.shape)
    base_index = 2 * expert_range[None, :] * expert_rows + ranking
    spill_index = local_count * expert_rows
    target_lower = jnp.where(chosen, base_index, spill_index)
    target_upper = jnp.where(chosen, base_index + expert_rows, spill_index)
    source_slot = jnp.zeros((spill_index,), jnp.int32)
    source_slot = source_slot.at[target_lower.reshape(-1)].set(slot_index.reshape(-1), mode="drop")
    source_slot = source_slot.at[target_upper.reshape(-1)].set(slot_index.reshape(-1), mode="drop")
    outgoing = arrived[source_slot].reshape(local_count, expert_rows, model_width)
    received = lax.all_to_all(outgoing, "loc", split_axis=0, concat_axis=0, tiled=True)
    flat_rows = received.reshape(-1, model_width)
    gate_act = jnp.dot(flat_rows, w_gate[0], preferred_element_type=jnp.float32)
    up_act = jnp.dot(flat_rows, w_up[0], preferred_element_type=jnp.float32)
    hidden = (jax.nn.silu(gate_act) * up_act).astype(jnp.bfloat16)
    hidden = hidden.reshape(local_count, expert_rows, w_gate.shape[2])
    own_hidden = lax.dynamic_slice_in_dim(hidden, own_half * half_rows, half_rows, 1)
    given_hidden = lax.dynamic_slice_in_dim(hidden, (1 - own_half) * half_rows, half_rows, 1)
    taken_hidden, other_down = from_partner((given_hidden, w_down[0]), "loc", 0)
    hidden_full = ordered_pair(own_hidden, taken_hidden, is_lower, 2)
    down_full = ordered_pair(w_down[0], other_down, is_lower, 0)
    result = jnp.dot(
        hidden_full.reshape(-1, hidden_full.shape[2]), down_full, preferred_element_type=jnp.float32
    )
    result = result.astype(jnp.bfloat16).reshape(local_count, half_rows, model_width)
    returned = lax.all_to_all(result, "loc", split_axis=0, concat_axis=0, tiled=True)
    flat_returned = returned.reshape(-1, model_width)
    filled_slot = jnp.any(inside, axis=1)
    first_pick = jnp.argmax(inside, axis=1)
    second_pick = top_count - 1 - jnp.argmax(inside[:, ::-1], axis=1)

    def pick_term(which):
        local_pick = jnp.take_along_axis(local_ids, which[:, None], axis=1)[:, 0]
        local_pick = jnp.where(filled_slot, local_pick, 0)
        rank_pick = jnp.take_along_axis(ranking, local_pick[:, None], axis=1)[:, 0]
        row_pick = (2 * local_pick + rank_pick // half_rows) * half_rows + rank_pick % half_rows
        row_pick = jnp.where(filled_slot, row_pick, 0)
        weight = jnp.take_along_axis(arrived_nums, which[:, None], axis=1)[:, 0]
        weight = jnp.where(filled_slot, weight, 0).astype(jnp.float32) / denominator
        return weight[:, None] * flat_returned[row_pick].astype(jnp.float32)

    group_sum = (pick_term(first_pick) + pick_term(second_pick)).astype(jnp.bfloat16)
    group_sum = group_sum.reshape(group_count, capacity, model_width)
    returned_sums = lax.all_to_all(group_sum, "grp", split_axis=0, concat_axis=0, tiled=True)
    mixed_sum = jnp.dot(
        dispatch_matrix.T,
        returned_sums.reshape(slots_all, model_width),
        preferred_element_type=jnp.float32,
    )
    return (inputs_float + mixed_sum).astype(jnp.bfloat16)


MESH = pl.DeviceIdType.MESH
Z, X, Y, S, FA, FB, R1, R2A, R2B, R3X, R3Y, R4 = 0, 1, 2, 3, 7, 8, 9, 13, 14, 15, 16, 17
KINDS = 18


def flip(value, bit, unit):
    digit = (value // unit) % 2
    return value + unit * ((digit + bit) % 2 - digit)


def fused_kernel(
    tokens_ref, gain_ref, w_gate_ref, w_up_ref, w_down_ref, ids_ref, nums_ref, out_ref,
    rows, sums, from_sibling, diag_in, near_in, z_in, w_in, num_all,
    send_sem, recv_sem, z_send, num_send, num_recv,
):
    grp, loc = lax.axis_index("grp"), lax.axis_index("loc")
    n_rows, width = tokens_ref.shape
    half = n_rows // 2
    hidden_units = w_gate_ref.shape[2]
    experts = num_all.shape[1]
    sibling = (flip(grp, 1, 1), loc)
    along_x = (flip(grp, 1, 2), loc)
    along_y = (flip(grp, 1, 4), loc)
    me = grp * 4 + loc
    everyone = 32
    upper = loc // 2
    mirrored = loc + upper * (3 - 2 * loc)
    outer, inner, far_inner = 3 * upper, 1 + upper, 2 - upper

    def plane(i):
        from_end = (i // 2) * i + (1 - i // 2) * ((mirrored + i) % 2)
        return from_end + upper * (3 - 2 * from_end)

    def worked(k):
        return plane((k + 1) % 4)

    barrier = pltpu.get_barrier_semaphore()

    @pl.loop(1, everyone)
    def _(i):
        other = (me + i) % everyone
        pl.semaphore_signal(barrier, 1, device_id=(other // 4, other % 4), device_id_type=MESH)

    inputs = tokens_ref[...].astype(jnp.float32)
    inv_scale = lax.rsqrt(jnp.mean(inputs * inputs, axis=-1, keepdims=True) + epsilon)
    rows[4 * loc, pl.ds(0, n_rows), :] = (
        inputs * inv_scale * gain_ref[...].astype(jnp.float32)
    ).astype(jnp.bfloat16)
    expert_row = lax.broadcasted_iota(jnp.int32, (experts, n_rows), 0)
    numerators = jnp.zeros((experts, n_rows), jnp.int32)
    for k in range(ids_ref.shape[0]):
        numerators += jnp.where(ids_ref[k : k + 1, :] == expert_row, nums_ref[k : k + 1, :], 0)
    num_all[me] = numerators.astype(jnp.float32).astype(jnp.bfloat16)
    pl.semaphore_wait(barrier, everyone - 1)

    def remote(kind, j, source, target, device):
        return pltpu.make_async_remote_copy(
            src_ref=source,
            dst_ref=target,
            send_sem=send_sem.at[kind * 4 + j],
            recv_sem=recv_sem.at[kind * 4 + j],
            device_id=device,
            device_id_type=MESH,
        )

    own, other_core = pl.ds(0, n_rows), pl.ds(n_rows, n_rows)
    first, second = pl.ds(0, half), pl.ds(half, half)

    def copy_z(j, index, target):
        return pltpu.make_async_remote_copy(
            src_ref=rows.at[4 * j, own],
            dst_ref=rows.at[4 * j, own],
            send_sem=z_send.at[index],
            recv_sem=recv_sem.at[Z * 4 + j],
            device_id=(grp, target),
            device_id_type=MESH,
        )

    def copy_x(j):
        return remote(X, j, rows.at[4 * j, own], rows.at[4 * j + 1, own], along_x)

    def copy_y(j):
        return remote(Y, j, rows.at[4 * j, own], rows.at[4 * j + 2, own], along_y)

    def copy_s(j, q):
        t = 4 * j + q
        return remote(S + q, j, rows.at[t, own], rows.at[t, other_core], sibling)

    def copy_fa(j):
        return remote(FA, j, rows.at[4 * j + 1, first], rows.at[4 * j + 3, first], along_y)

    def copy_fb(j):
        return remote(FB, j, rows.at[4 * j + 2, second], rows.at[4 * j + 3, second], along_x)

    def copy_r1(j, q):
        t = 4 * j + q
        return remote(R1 + q, j, rows.at[t, other_core], from_sibling.at[t], sibling)

    def copy_r2a(j):
        return remote(R2A, j, sums.at[4 * j + 3, first], diag_in.at[j, first], along_x)

    def copy_r2b(j):
        return remote(R2B, j, sums.at[4 * j + 3, second], diag_in.at[j, second], along_y)

    def copy_r3x(j):
        return remote(R3X, j, sums.at[4 * j + 1], near_in.at[j, 0], along_x)

    def copy_r3y(j):
        return remote(R3Y, j, sums.at[4 * j + 2], near_in.at[j, 1], along_y)

    def copy_r4(j):
        return pltpu.make_async_remote_copy(
            src_ref=sums.at[4 * j],
            dst_ref=z_in.at[loc],
            send_sem=send_sem.at[R4 * 4 + j],
            recv_sem=recv_sem.at[R4 * 4 + loc],
            device_id=(grp, j),
            device_id_type=MESH,
        )

    def arrival_r4(j):
        return pltpu.make_async_remote_copy(
            src_ref=z_in.at[j],
            dst_ref=z_in.at[j],
            send_sem=send_sem.at[R4 * 4 + j],
            recv_sem=recv_sem.at[R4 * 4 + j],
            device_id=(grp, j),
            device_id_type=MESH,
        )

    def numerator_copy(source, target, device):
        return pltpu.make_async_remote_copy(
            src_ref=source,
            dst_ref=target,
            send_sem=num_send,
            recv_sem=num_recv,
            device_id=device,
            device_id_type=MESH,
        )

    def spread(j):
        copy_x(j).start()
        copy_y(j).start()
        copy_s(j, 0).start()

    def forward(j):
        copy_x(j).wait_recv()
        copy_fa(j).start()
        copy_s(j, 1).start()
        copy_y(j).wait_recv()
        copy_fb(j).start()
        copy_s(j, 2).start()

    def forward_diagonal(j):
        copy_fa(j).wait_recv()
        copy_fb(j).wait_recv()
        copy_s(j, 3).start()

    def add(t, extra=(), place=None):
        place = pl.ds(0, n_rows) if place is None else place
        total = sums[t, place, :].astype(jnp.float32)
        total += from_sibling[t, place, :].astype(jnp.float32)
        for term in extra:
            total += term[place, :].astype(jnp.float32)
        sums[t, place, :] = total.astype(jnp.bfloat16)

    def reduce_diagonal(j):
        copy_r1(j, 3).wait_recv()
        add(4 * j + 3)
        copy_r2a(j).start()
        copy_r2b(j).start()

    def reduce_near(j):
        copy_r1(j, 1).wait_recv()
        add(4 * j + 1, (), first)
        copy_r2b(j).wait_recv()
        add(4 * j + 1, (diag_in.at[j],), second)
        copy_r3x(j).start()
        copy_r1(j, 2).wait_recv()
        add(4 * j + 2, (), second)
        copy_r2a(j).wait_recv()
        add(4 * j + 2, (diag_in.at[j],), first)
        copy_r3y(j).start()

    def reduce_plane(j):
        copy_r1(j, 0).wait_recv()
        copy_r3x(j).wait_recv()
        copy_r3y(j).wait_recv()
        add(4 * j, (near_in.at[j, 0], near_in.at[j, 1]))

    is_inner = mirrored == 1

    def take_plane(i, target):
        copy_z(plane(i), 1 + i, target).wait_recv()

        @pl.when(is_inner)
        def _():
            copy_z(plane(i), 1 + i, target).start()

        spread(plane(i))

    @pl.when(is_inner)
    def _():
        copy_z(loc, 0, outer).start()
        copy_z(loc, 1, far_inner).start()

    @pl.when(mirrored == 0)
    def _():
        copy_z(loc, 0, inner).start()

    spread(loc)

    @pl.loop(1, everyone)
    def _(i):
        other = (me + i) % everyone
        numerator_copy(num_all.at[me], num_all.at[me], (other // 4, other % 4)).start()

    w_in[:, :hidden_units] = w_gate_ref[0]
    w_in[:, hidden_units:] = w_up_ref[0]
    forward(loc)
    take_plane(1, far_inner)
    take_plane(2, outer)
    forward_diagonal(loc)
    forward(plane(1))
    take_plane(3, outer)
    numerator_copy(
        num_all.at[pl.ds(0, everyone - 1)], num_all.at[pl.ds(0, everyone - 1)], sibling
    ).wait_recv()

    own_expert = grp * 2 + loc // 2
    pick = (expert_row == own_expert).astype(jnp.float32).astype(jnp.bfloat16)

    def weights_of(j, q, core_flip):
        source = flip(flip(flip(grp, core_flip, 1), q % 2, 2), q // 2, 4)
        place = source * 4 + j
        return lax.dot_general(
            num_all[place], pick, (((0,), (0,)), ((), ())), preferred_element_type=jnp.float32
        )[:, :1] * (1.0 / denominator)

    @pl.loop(0, 16)
    def _(step):
        k, q = step // 4, step % 4
        j = worked(k)
        t = 4 * j + q

        @pl.when(q == 0)
        def _():
            @pl.when(k >= 2)
            def _():
                reduce_plane(worked(k - 2))
                copy_r4(worked(k - 2)).start()

            copy_s(j, 0).wait_recv()

        @pl.when(q == 1)
        def _():
            @pl.when(k >= 1)
            def _():
                reduce_diagonal(worked(k - 1))

            @pl.when(k < 3)
            def _():
                forward_diagonal(j)

            copy_s(j, 1).wait_recv()

        @pl.when(q == 2)
        def _():
            @pl.when(k >= 1)
            def _():
                reduce_near(worked(k - 1))

            copy_s(j, 2).wait_recv()

        @pl.when(q == 3)
        def _():
            @pl.when(k < 2)
            def _():
                forward(plane(k + 2))

            copy_s(j, 3).wait_recv()

        both = jnp.dot(rows[t], w_in[...], preferred_element_type=jnp.float32)
        gate_act, up_act = both[:, :hidden_units], both[:, hidden_units:]
        hidden = (jax.nn.silu(gate_act) * up_act).astype(jnp.bfloat16)
        weight = jnp.concatenate([weights_of(j, q, 0), weights_of(j, q, 1)], axis=0)
        piece = width // 4
        for part in range(4):
            columns = pl.ds(part * piece, piece)
            result = jnp.dot(
                hidden, w_down_ref[0, :, columns], preferred_element_type=jnp.float32
            )
            result = (result * weight).astype(jnp.bfloat16)
            sums[t, :, columns] = result[:n_rows]
            rows[t, other_core, columns] = result[n_rows:]
        for which in range(4):
            @pl.when(q == which)
            def _():
                copy_r1(j, which).start()

    reduce_diagonal(loc)
    reduce_plane(worked(2))
    copy_r4(worked(2)).start()
    reduce_near(loc)
    reduce_plane(loc)
    total = tokens_ref[...].astype(jnp.float32) + sums[4 * loc].astype(jnp.float32)
    for i in (1, 2, 3):
        arrival_r4(plane(i)).wait_recv()
        total += z_in[plane(i)].astype(jnp.float32)
    out_ref[...] = total.astype(jnp.bfloat16)

    copy_z(loc, 0, outer).wait_send()

    @pl.when(is_inner)
    def _():
        copy_z(loc, 1, far_inner).wait_send()
        for i in (1, 2, 3):
            copy_z(plane(i), 1 + i, outer).wait_send()

    for i in (1, 2, 3):
        copy_r4(plane(i)).wait_send()

    @pl.loop(0, 4)
    def _(j):
        copy_x(j).wait_send()
        copy_y(j).wait_send()
        for q in range(4):
            copy_s(j, q).wait_send()
            copy_r1(j, q).wait_send()
        for make in (copy_fa, copy_fb, copy_r2a, copy_r2b, copy_r3x, copy_r3y):
            make(j).wait_send()

    numerator_copy(
        num_all.at[pl.ds(0, everyone - 1)], num_all.at[pl.ds(0, everyone - 1)], sibling
    ).wait_send()


def fused(tokens, norm_gain, w_gate, w_up, w_down, expert_ids, gate_num):
    n_rows, width = tokens.shape
    hidden_units = w_gate.shape[2]
    bf16 = jnp.bfloat16
    return pl.pallas_call(
        fused_kernel,
        out_shape=jax.ShapeDtypeStruct(tokens.shape, tokens.dtype),
        in_specs=[pl.BlockSpec(memory_space=pltpu.VMEM)] * 7,
        out_specs=pl.BlockSpec(memory_space=pltpu.VMEM),
        scratch_shapes=[
            pltpu.VMEM((16, 2 * n_rows, width), bf16),
            pltpu.VMEM((16, n_rows, width), bf16),
            pltpu.VMEM((16, n_rows, width), bf16),
            pltpu.VMEM((4, n_rows, width), bf16),
            pltpu.VMEM((4, 2, n_rows, width), bf16),
            pltpu.VMEM((4, n_rows, width), bf16),
            pltpu.VMEM((width, 2 * hidden_units), bf16),
            pltpu.VMEM((32, 16, n_rows), bf16),
            pltpu.SemaphoreType.DMA((KINDS * 4,)),
            pltpu.SemaphoreType.DMA((KINDS * 4,)),
            pltpu.SemaphoreType.DMA((5,)),
            pltpu.SemaphoreType.DMA,
            pltpu.SemaphoreType.DMA,
        ],
        compiler_params=pltpu.CompilerParams(
            collective_id=0, has_side_effects=True, vmem_limit_bytes=60 * 2**20
        ),
        cost_estimate=pl.CostEstimate(
            flops=2 * 32 * n_rows * width * hidden_units * 3,
            bytes_accessed=2 * width * hidden_units * 3,
            transcendentals=32 * n_rows * hidden_units,
        ),
    )(tokens, norm_gain.reshape(1, width), w_gate, w_up, w_down, expert_ids.T, gate_num.T)


def shards(tokens, *others):
    if (lax.axis_size("grp"), lax.axis_size("loc")) == (8, 4):
        return fused(tokens, *others)
    return routed(tokens, *others)


def solution(mesh):
    return jax.shard_map(
        shards,
        mesh=mesh,
        in_specs=(
            P(("grp", "loc"), None),
            P(),
            P(("grp", "loc"), None, None),
            P(("grp", "loc"), None, None),
            P(("grp", "loc"), None, None),
            P(("grp", "loc"), None),
            P(("grp", "loc"), None),
        ),
        out_specs=P(("grp", "loc"), None),
        check_vma=False,
    )
```

```python
import jax
import jax.numpy as jnp
from jax import lax
from jax.experimental import pallas as pl
from jax.experimental.pallas import tpu as pltpu
from jax.sharding import PartitionSpec as P

GTOP = 4


epsilon = 1e-06
denominator = 1024.0


def from_partner(value, axis, apart):
    mask = 2**apart
    pairs = [(source, source ^ mask) for source in range(lax.axis_size(axis))]
    return lax.ppermute(value, axis, pairs)


def ordered_pair(own_part, other_part, is_lower, axis_index):
    lower_part = jnp.where(is_lower, own_part, other_part)
    upper_part = jnp.where(is_lower, other_part, own_part)
    return jnp.concatenate([lower_part, upper_part], axis=axis_index)


def routed(tokens, norm_gain, w_gate, w_up, w_down, expert_ids, gate_num):
    group_count = lax.axis_size("grp")
    local_count = lax.axis_size("loc")
    rows_dev, model_width = tokens.shape
    top_count = expert_ids.shape[1]
    experts_group = local_count // 2
    capacity = 2 * rows_dev * GTOP // group_count
    expert_rows = rows_dev * GTOP * (top_count // GTOP) // experts_group
    half_rows = expert_rows // 2
    slots_all = group_count * capacity
    inputs_float = tokens.astype(jnp.float32)
    inv_scale = lax.rsqrt(jnp.mean(inputs_float * inputs_float, axis=-1, keepdims=True) + epsilon)
    normed = (inputs_float * inv_scale * norm_gain.astype(jnp.float32)).astype(jnp.bfloat16)
    owner_group = expert_ids // experts_group
    group_range = jnp.arange(group_count, dtype=jnp.int32)
    member = jnp.any(owner_group[:, :, None] == group_range[None, None, :], axis=1)
    position = jnp.cumsum(member.astype(jnp.int32), axis=0) - 1
    slot_range = jnp.arange(capacity, dtype=jnp.int32)
    slot_table = member.T[:, None, :] & (position.T[:, None, :] == slot_range[None, :, None])
    dispatch_matrix = slot_table.reshape(slots_all, rows_dev).astype(jnp.bfloat16)
    packed = jnp.dot(dispatch_matrix, normed, preferred_element_type=jnp.float32).astype(
        jnp.bfloat16
    )
    packed = packed.reshape(group_count, capacity, model_width)
    filled = jnp.any(slot_table, axis=2).reshape(slots_all)
    token_range = jnp.arange(rows_dev, dtype=jnp.int32)
    source_token = jnp.sum(
        slot_table.astype(jnp.int32) * token_range[None, None, :], axis=2
    ).reshape(slots_all)
    details = jnp.concatenate([expert_ids, gate_num], axis=1)[source_token]
    details = jnp.where(filled[:, None], details, -1).astype(jnp.bfloat16)
    details = details.reshape(group_count, capacity, 2 * top_count)
    arrived, arrived_details = (
        lax.all_to_all(packed, "grp", split_axis=0, concat_axis=0, tiled=True),
        lax.all_to_all(details, "grp", split_axis=0, concat_axis=0, tiled=True),
    )
    arrived = arrived.reshape(slots_all, model_width)
    arrived_details = arrived_details.reshape(slots_all, 2 * top_count).astype(jnp.int32)
    own_group = lax.axis_index("grp")
    own_half = lax.axis_index("loc") % 2
    is_lower = own_half == 0
    arrived_ids = arrived_details[:, :top_count]
    arrived_nums = arrived_details[:, top_count:]
    local_ids = arrived_ids - own_group * experts_group
    inside = (arrived_ids >= 0) & (local_ids >= 0) & (local_ids < experts_group)
    expert_range = jnp.arange(experts_group, dtype=jnp.int32)
    chosen = jnp.any(
        inside[:, :, None] & (local_ids[:, :, None] == expert_range[None, None, :]), axis=1
    )
    ranking = jnp.cumsum(chosen.astype(jnp.int32), axis=0) - 1
    slot_index = jnp.broadcast_to(jnp.arange(slots_all, dtype=jnp.int32)[:, None], chosen.shape)
    base_index = 2 * expert_range[None, :] * expert_rows + ranking
    spill_index = local_count * expert_rows
    target_lower = jnp.where(chosen, base_index, spill_index)
    target_upper = jnp.where(chosen, base_index + expert_rows, spill_index)
    source_slot = jnp.zeros((spill_index,), jnp.int32)
    source_slot = source_slot.at[target_lower.reshape(-1)].set(slot_index.reshape(-1), mode="drop")
    source_slot = source_slot.at[target_upper.reshape(-1)].set(slot_index.reshape(-1), mode="drop")
    outgoing = arrived[source_slot].reshape(local_count, expert_rows, model_width)
    received = lax.all_to_all(outgoing, "loc", split_axis=0, concat_axis=0, tiled=True)
    flat_rows = received.reshape(-1, model_width)
    gate_act = jnp.dot(flat_rows, w_gate[0], preferred_element_type=jnp.float32)
    up_act = jnp.dot(flat_rows, w_up[0], preferred_element_type=jnp.float32)
    hidden = (jax.nn.silu(gate_act) * up_act).astype(jnp.bfloat16)
    hidden = hidden.reshape(local_count, expert_rows, w_gate.shape[2])
    own_hidden = lax.dynamic_slice_in_dim(hidden, own_half * half_rows, half_rows, 1)
    given_hidden = lax.dynamic_slice_in_dim(hidden, (1 - own_half) * half_rows, half_rows, 1)
    taken_hidden, other_down = from_partner((given_hidden, w_down[0]), "loc", 0)
    hidden_full = ordered_pair(own_hidden, taken_hidden, is_lower, 2)
    down_full = ordered_pair(w_down[0], other_down, is_lower, 0)
    result = jnp.dot(
        hidden_full.reshape(-1, hidden_full.shape[2]), down_full, preferred_element_type=jnp.float32
    )
    result = result.astype(jnp.bfloat16).reshape(local_count, half_rows, model_width)
    returned = lax.all_to_all(result, "loc", split_axis=0, concat_axis=0, tiled=True)
    flat_returned = returned.reshape(-1, model_width)
    filled_slot = jnp.any(inside, axis=1)
    first_pick = jnp.argmax(inside, axis=1)
    second_pick = top_count - 1 - jnp.argmax(inside[:, ::-1], axis=1)

    def pick_term(which):
        local_pick = jnp.take_along_axis(local_ids, which[:, None], axis=1)[:, 0]
        local_pick = jnp.where(filled_slot, local_pick, 0)
        rank_pick = jnp.take_along_axis(ranking, local_pick[:, None], axis=1)[:, 0]
        row_pick = (2 * local_pick + rank_pick // half_rows) * half_rows + rank_pick % half_rows
        row_pick = jnp.where(filled_slot, row_pick, 0)
        weight = jnp.take_along_axis(arrived_nums, which[:, None], axis=1)[:, 0]
        weight = jnp.where(filled_slot, weight, 0).astype(jnp.float32) / denominator
        return weight[:, None] * flat_returned[row_pick].astype(jnp.float32)

    group_sum = (pick_term(first_pick) + pick_term(second_pick)).astype(jnp.bfloat16)
    group_sum = group_sum.reshape(group_count, capacity, model_width)
    returned_sums = lax.all_to_all(group_sum, "grp", split_axis=0, concat_axis=0, tiled=True)
    mixed_sum = jnp.dot(
        dispatch_matrix.T,
        returned_sums.reshape(slots_all, model_width),
        preferred_element_type=jnp.float32,
    )
    return (inputs_float + mixed_sum).astype(jnp.bfloat16)


MESH = pl.DeviceIdType.MESH
Z, X, Y, S, FA, FB, R1, R2A, R2B, R3X, R3Y, R4, D, RD = 0, 1, 2, 3, 7, 8, 9, 13, 14, 15, 16, 17, 18, 19
KINDS = 20


def flip(value, bit, unit):
    digit = (value // unit) % 2
    return value + unit * ((digit + bit) % 2 - digit)


def fused_kernel(
    tokens_ref, gain_ref, w_gate_ref, w_up_ref, w_down_ref, ids_ref, nums_ref, out_ref,
    rows, sums, from_sibling, diag_in, near_in, z_in, far_in, w_in, num_all,
    send_sem, recv_sem, z_send, num_send, num_recv,
):
    grp, loc = lax.axis_index("grp"), lax.axis_index("loc")
    n_rows, width = tokens_ref.shape
    half = n_rows // 2
    hidden_units = w_gate_ref.shape[2]
    experts = num_all.shape[1]
    sibling = (flip(grp, 1, 1), loc)
    along_x = (flip(grp, 1, 2), loc)
    along_y = (flip(grp, 1, 4), loc)
    me = grp * 4 + loc
    everyone = 32
    upper = loc // 2
    mirrored = loc + upper * (3 - 2 * loc)
    outer, inner, far_inner = 3 * upper, 1 + upper, 2 - upper

    def plane(i):
        from_end = (i // 2) * i + (1 - i // 2) * ((mirrored + i) % 2)
        return from_end + upper * (3 - 2 * from_end)

    def worked(k):
        return plane((k + 1) % 4)

    barrier = pltpu.get_barrier_semaphore()

    @pl.loop(1, everyone)
    def _(i):
        other = (me + i) % everyone
        pl.semaphore_signal(barrier, 1, device_id=(other // 4, other % 4), device_id_type=MESH)

    inputs = tokens_ref[...].astype(jnp.float32)
    inv_scale = lax.rsqrt(jnp.mean(inputs * inputs, axis=-1, keepdims=True) + epsilon)
    rows[4 * loc, pl.ds(0, n_rows), :] = (
        inputs * inv_scale * gain_ref[...].astype(jnp.float32)
    ).astype(jnp.bfloat16)
    expert_row = lax.broadcasted_iota(jnp.int32, (experts, n_rows), 0)
    numerators = jnp.zeros((experts, n_rows), jnp.int32)
    for k in range(ids_ref.shape[0]):
        numerators += jnp.where(ids_ref[k : k + 1, :] == expert_row, nums_ref[k : k + 1, :], 0)
    num_all[me] = numerators.astype(jnp.float32).astype(jnp.bfloat16)
    pl.semaphore_wait(barrier, everyone - 1)

    def remote(kind, j, source, target, device):
        return pltpu.make_async_remote_copy(
            src_ref=source,
            dst_ref=target,
            send_sem=send_sem.at[kind * 4 + j],
            recv_sem=recv_sem.at[kind * 4 + j],
            device_id=device,
            device_id_type=MESH,
        )

    own, other_core = pl.ds(0, n_rows), pl.ds(n_rows, n_rows)
    first, second = pl.ds(0, half), pl.ds(half, half)

    def copy_z(j, index, target):
        return pltpu.make_async_remote_copy(
            src_ref=rows.at[4 * j, own],
            dst_ref=rows.at[4 * j, own],
            send_sem=z_send.at[index],
            recv_sem=recv_sem.at[Z * 4 + j],
            device_id=(grp, target),
            device_id_type=MESH,
        )

    def copy_d(j, index, target):
        return pltpu.make_async_remote_copy(
            src_ref=rows.at[4 * j + 3, own],
            dst_ref=rows.at[4 * j + 3, own],
            send_sem=z_send.at[5 + index],
            recv_sem=recv_sem.at[D * 4 + j],
            device_id=(grp, target),
            device_id_type=MESH,
        )

    def copy_rd(j):
        return pltpu.make_async_remote_copy(
            src_ref=sums.at[4 * j + 3],
            dst_ref=far_in.at[loc],
            send_sem=send_sem.at[RD * 4 + j],
            recv_sem=recv_sem.at[RD * 4 + loc],
            device_id=(grp, j),
            device_id_type=MESH,
        )

    def add_far(j):
        pltpu.make_async_remote_copy(
            src_ref=far_in.at[j],
            dst_ref=far_in.at[j],
            send_sem=send_sem.at[RD * 4 + j],
            recv_sem=recv_sem.at[RD * 4 + j],
            device_id=(grp, j),
            device_id_type=MESH,
        ).wait_recv()
        t = 4 * loc + 3
        total = sums[t].astype(jnp.float32) + far_in[j].astype(jnp.float32)
        sums[t] = total.astype(jnp.bfloat16)

    def copy_x(j):
        return remote(X, j, rows.at[4 * j, own], rows.at[4 * j + 1, own], along_x)

    def copy_y(j):
        return remote(Y, j, rows.at[4 * j, own], rows.at[4 * j + 2, own], along_y)

    def copy_s(j, q):
        t = 4 * j + q
        return remote(S + q, j, rows.at[t, own], rows.at[t, other_core], sibling)

    def copy_fa(j):
        return remote(FA, j, rows.at[4 * j + 1, first], rows.at[4 * j + 3, first], along_y)

    def copy_fb(j):
        return remote(FB, j, rows.at[4 * j + 2, second], rows.at[4 * j + 3, second], along_x)

    def copy_r1(j, q):
        t = 4 * j + q
        return remote(R1 + q, j, rows.at[t, other_core], from_sibling.at[t], sibling)

    def copy_r2a(j):
        return remote(R2A, j, sums.at[4 * j + 3, first], diag_in.at[j, first], along_x)

    def copy_r2b(j):
        return remote(R2B, j, sums.at[4 * j + 3, second], diag_in.at[j, second], along_y)

    def copy_r3x(j):
        return remote(R3X, j, sums.at[4 * j + 1], near_in.at[j, 0], along_x)

    def copy_r3y(j):
        return remote(R3Y, j, sums.at[4 * j + 2], near_in.at[j, 1], along_y)

    def copy_r4(j):
        return pltpu.make_async_remote_copy(
            src_ref=sums.at[4 * j],
            dst_ref=z_in.at[loc],
            send_sem=send_sem.at[R4 * 4 + j],
            recv_sem=recv_sem.at[R4 * 4 + loc],
            device_id=(grp, j),
            device_id_type=MESH,
        )

    def arrival_r4(j):
        return pltpu.make_async_remote_copy(
            src_ref=z_in.at[j],
            dst_ref=z_in.at[j],
            send_sem=send_sem.at[R4 * 4 + j],
            recv_sem=recv_sem.at[R4 * 4 + j],
            device_id=(grp, j),
            device_id_type=MESH,
        )

    def numerator_copy(source, target, device):
        return pltpu.make_async_remote_copy(
            src_ref=source,
            dst_ref=target,
            send_sem=num_send,
            recv_sem=num_recv,
            device_id=device,
            device_id_type=MESH,
        )

    def spread(j):
        copy_x(j).start()
        copy_y(j).start()
        copy_s(j, 0).start()

    def forward(j, diagonal):
        copy_x(j).wait_recv()
        if diagonal:
            copy_fa(j).start()
        copy_s(j, 1).start()
        copy_y(j).wait_recv()
        if diagonal:
            copy_fb(j).start()
        copy_s(j, 2).start()

    def take_diagonal(i):
        copy_d(plane(i), 2, outer).wait_recv()
        copy_s(plane(i), 3).start()

    def forward_diagonal(j):
        copy_fa(j).wait_recv()
        copy_fb(j).wait_recv()
        copy_s(j, 3).start()

    def add(t, extra=(), place=None):
        place = pl.ds(0, n_rows) if place is None else place
        total = sums[t, place, :].astype(jnp.float32)
        total += from_sibling[t, place, :].astype(jnp.float32)
        for term in extra:
            total += term[place, :].astype(jnp.float32)
        sums[t, place, :] = total.astype(jnp.bfloat16)

    def reduce_diagonal(j):
        copy_r2a(j).start()
        copy_r2b(j).start()

    def add_sibling(j):
        copy_r1(j, 3).wait_recv()
        add(4 * j + 3)

    def reduce_near(j):
        copy_r1(j, 1).wait_recv()
        add(4 * j + 1, (), first)
        copy_r2b(j).wait_recv()
        add(4 * j + 1, (diag_in.at[j],), second)
        copy_r3x(j).start()
        copy_r1(j, 2).wait_recv()
        add(4 * j + 2, (), second)
        copy_r2a(j).wait_recv()
        add(4 * j + 2, (diag_in.at[j],), first)
        copy_r3y(j).start()

    def reduce_near_only(j):
        copy_r1(j, 1).wait_recv()
        add(4 * j + 1)
        copy_r3x(j).start()
        copy_r1(j, 2).wait_recv()
        add(4 * j + 2)
        copy_r3y(j).start()

    def reduce_plane(j):
        copy_r1(j, 0).wait_recv()
        copy_r3x(j).wait_recv()
        copy_r3y(j).wait_recv()
        add(4 * j, (near_in.at[j, 0], near_in.at[j, 1]))

    is_inner = mirrored == 1

    def take_plane(i, target):
        copy_z(plane(i), 1 + i, target).wait_recv()

        @pl.when(is_inner)
        def _():
            copy_z(plane(i), 1 + i, target).start()

        spread(plane(i))

    @pl.when(is_inner)
    def _():
        copy_z(loc, 0, outer).start()
        copy_z(loc, 1, far_inner).start()

    @pl.when(mirrored == 0)
    def _():
        copy_z(loc, 0, inner).start()

    spread(loc)

    @pl.loop(1, everyone)
    def _(i):
        other = (me + i) % everyone
        numerator_copy(num_all.at[me], num_all.at[me], (other // 4, other % 4)).start()

    w_in[:, :hidden_units] = w_gate_ref[0]
    w_in[:, hidden_units:] = w_up_ref[0]
    forward(loc, True)
    take_plane(1, far_inner)
    take_plane(2, outer)
    forward_diagonal(loc)

    @pl.when(is_inner)
    def _():
        copy_d(loc, 0, outer).start()
        copy_d(loc, 1, far_inner).start()

    @pl.when(mirrored == 0)
    def _():
        copy_d(loc, 0, inner).start()

    forward(plane(1), False)
    take_plane(3, outer)
    numerator_copy(
        num_all.at[pl.ds(0, everyone - 1)], num_all.at[pl.ds(0, everyone - 1)], sibling
    ).wait_recv()

    own_expert = grp * 2 + loc // 2
    pick = (expert_row == own_expert).astype(jnp.float32).astype(jnp.bfloat16)

    def weights_of(j, q, core_flip):
        source = flip(flip(flip(grp, core_flip, 1), q % 2, 2), q // 2, 4)
        place = source * 4 + j
        return lax.dot_general(
            num_all[place], pick, (((0,), (0,)), ((), ())), preferred_element_type=jnp.float32
        )[:, :1] * (1.0 / denominator)

    @pl.loop(0, 16)
    def _(step):
        k, q = step // 4, step % 4
        j = worked(k)
        t = 4 * j + q

        @pl.when(q == 0)
        def _():
            @pl.when(k >= 2)
            def _():
                reduce_plane(worked(k - 2))
                copy_r4(worked(k - 2)).start()

            copy_s(j, 0).wait_recv()

        @pl.when(q == 1)
        def _():
            @pl.when(k >= 1)
            def _():
                add_sibling(worked(k - 1))

                @pl.when(k < 3)
                def _():
                    copy_rd(worked(k - 1)).start()

                @pl.when(k == 3)
                def _():
                    reduce_diagonal(worked(k - 1))

            @pl.when(k == 0)
            def _():
                take_diagonal(1)

                @pl.when(is_inner)
                def _():
                    take_diagonal(2)
                    copy_d(plane(2), 2, outer).start()

            @pl.when((k == 1) & (mirrored == 0))
            def _():
                take_diagonal(2)

            @pl.when(k == 2)
            def _():
                forward_diagonal(j)

            copy_s(j, 1).wait_recv()

        @pl.when(q == 2)
        def _():
            @pl.when((k >= 1) & (k < 3))
            def _():
                reduce_near_only(worked(k - 1))

            @pl.when(k == 3)
            def _():
                reduce_near(worked(k - 1))

            copy_s(j, 2).wait_recv()

        @pl.when(q == 3)
        def _():
            @pl.when(k == 0)
            def _():
                forward(plane(2), False)

            @pl.when(k == 1)
            def _():
                forward(plane(3), True)

            copy_s(j, 3).wait_recv()

        both = jnp.dot(rows[t], w_in[...], preferred_element_type=jnp.float32)
        gate_act, up_act = both[:, :hidden_units], both[:, hidden_units:]
        hidden = (jax.nn.silu(gate_act) * up_act).astype(jnp.bfloat16)
        weight = jnp.concatenate([weights_of(j, q, 0), weights_of(j, q, 1)], axis=0)
        piece = width // 4
        for part in range(4):
            columns = pl.ds(part * piece, piece)
            result = jnp.dot(
                hidden, w_down_ref[0, :, columns], preferred_element_type=jnp.float32
            )
            result = (result * weight).astype(jnp.bfloat16)
            sums[t, :, columns] = result[:n_rows]
            rows[t, other_core, columns] = result[n_rows:]
        for which in range(4):
            @pl.when(q == which)
            def _():
                copy_r1(j, which).start()

    add_sibling(loc)

    @pl.when(is_inner)
    def _():
        for i in (1, 2, 3):
            add_far(plane(i))

    @pl.when(mirrored == 0)
    def _():
        add_far(plane(1))

    reduce_diagonal(loc)
    reduce_plane(worked(2))
    copy_r4(worked(2)).start()
    reduce_near(loc)
    reduce_plane(loc)
    total = tokens_ref[...].astype(jnp.float32) + sums[4 * loc].astype(jnp.float32)
    for i in (1, 2, 3):
        arrival_r4(plane(i)).wait_recv()
        total += z_in[plane(i)].astype(jnp.float32)
    out_ref[...] = total.astype(jnp.bfloat16)

    copy_z(loc, 0, outer).wait_send()
    copy_d(loc, 0, outer).wait_send()
    for i in (1, 2):
        copy_rd(plane(i)).wait_send()
    for j in (loc, plane(3)):
        for make in (copy_fa, copy_fb, copy_r2a, copy_r2b):
            make(j).wait_send()

    @pl.when(is_inner)
    def _():
        copy_z(loc, 1, far_inner).wait_send()
        copy_d(loc, 1, far_inner).wait_send()
        copy_d(plane(2), 2, outer).wait_send()
        for i in (1, 2, 3):
            copy_z(plane(i), 1 + i, outer).wait_send()

    for i in (1, 2, 3):
        copy_r4(plane(i)).wait_send()

    @pl.loop(0, 4)
    def _(j):
        copy_x(j).wait_send()
        copy_y(j).wait_send()
        for q in range(4):
            copy_s(j, q).wait_send()
            copy_r1(j, q).wait_send()
        copy_r3x(j).wait_send()
        copy_r3y(j).wait_send()

    numerator_copy(
        num_all.at[pl.ds(0, everyone - 1)], num_all.at[pl.ds(0, everyone - 1)], sibling
    ).wait_send()


def fused(tokens, norm_gain, w_gate, w_up, w_down, expert_ids, gate_num):
    n_rows, width = tokens.shape
    hidden_units = w_gate.shape[2]
    bf16 = jnp.bfloat16
    return pl.pallas_call(
        fused_kernel,
        out_shape=jax.ShapeDtypeStruct(tokens.shape, tokens.dtype),
        in_specs=[pl.BlockSpec(memory_space=pltpu.VMEM)] * 7,
        out_specs=pl.BlockSpec(memory_space=pltpu.VMEM),
        scratch_shapes=[
            pltpu.VMEM((16, 2 * n_rows, width), bf16),
            pltpu.VMEM((16, n_rows, width), bf16),
            pltpu.VMEM((16, n_rows, width), bf16),
            pltpu.VMEM((4, n_rows, width), bf16),
            pltpu.VMEM((4, 2, n_rows, width), bf16),
            pltpu.VMEM((4, n_rows, width), bf16),
            pltpu.VMEM((4, n_rows, width), bf16),
            pltpu.VMEM((width, 2 * hidden_units), bf16),
            pltpu.VMEM((32, 16, n_rows), bf16),
            pltpu.SemaphoreType.DMA((KINDS * 4,)),
            pltpu.SemaphoreType.DMA((KINDS * 4,)),
            pltpu.SemaphoreType.DMA((8,)),
            pltpu.SemaphoreType.DMA,
            pltpu.SemaphoreType.DMA,
        ],
        compiler_params=pltpu.CompilerParams(
            collective_id=0, has_side_effects=True, vmem_limit_bytes=60 * 2**20
        ),
        cost_estimate=pl.CostEstimate(
            flops=2 * 32 * n_rows * width * hidden_units * 3,
            bytes_accessed=2 * width * hidden_units * 3,
            transcendentals=32 * n_rows * hidden_units,
        ),
    )(tokens, norm_gain.reshape(1, width), w_gate, w_up, w_down, expert_ids.T, gate_num.T)


def shards(tokens, *others):
    if (lax.axis_size("grp"), lax.axis_size("loc")) == (8, 4):
        return fused(tokens, *others)
    return routed(tokens, *others)


def solution(mesh):
    return jax.shard_map(
        shards,
        mesh=mesh,
        in_specs=(
            P(("grp", "loc"), None),
            P(),
            P(("grp", "loc"), None, None),
            P(("grp", "loc"), None, None),
            P(("grp", "loc"), None, None),
            P(("grp", "loc"), None),
            P(("grp", "loc"), None),
        ),
        out_specs=P(("grp", "loc"), None),
        check_vma=False,
    )
```

```python
import jax
import jax.numpy as jnp
from jax import lax
from jax.experimental import pallas as pl
from jax.experimental.pallas import tpu as pltpu
from jax.sharding import PartitionSpec as P

GTOP = 4


epsilon = 1e-06
denominator = 1024.0


def from_partner(value, axis, apart):
    mask = 2**apart
    pairs = [(source, source ^ mask) for source in range(lax.axis_size(axis))]
    return lax.ppermute(value, axis, pairs)


def ordered_pair(own_part, other_part, is_lower, axis_index):
    lower_part = jnp.where(is_lower, own_part, other_part)
    upper_part = jnp.where(is_lower, other_part, own_part)
    return jnp.concatenate([lower_part, upper_part], axis=axis_index)


def routed(tokens, norm_gain, w_gate, w_up, w_down, expert_ids, gate_num):
    group_count = lax.axis_size("grp")
    local_count = lax.axis_size("loc")
    rows_dev, model_width = tokens.shape
    top_count = expert_ids.shape[1]
    experts_group = local_count // 2
    capacity = 2 * rows_dev * GTOP // group_count
    expert_rows = rows_dev * GTOP * (top_count // GTOP) // experts_group
    half_rows = expert_rows // 2
    slots_all = group_count * capacity
    inputs_float = tokens.astype(jnp.float32)
    inv_scale = lax.rsqrt(jnp.mean(inputs_float * inputs_float, axis=-1, keepdims=True) + epsilon)
    normed = (inputs_float * inv_scale * norm_gain.astype(jnp.float32)).astype(jnp.bfloat16)
    owner_group = expert_ids // experts_group
    group_range = jnp.arange(group_count, dtype=jnp.int32)
    member = jnp.any(owner_group[:, :, None] == group_range[None, None, :], axis=1)
    position = jnp.cumsum(member.astype(jnp.int32), axis=0) - 1
    slot_range = jnp.arange(capacity, dtype=jnp.int32)
    slot_table = member.T[:, None, :] & (position.T[:, None, :] == slot_range[None, :, None])
    dispatch_matrix = slot_table.reshape(slots_all, rows_dev).astype(jnp.bfloat16)
    packed = jnp.dot(dispatch_matrix, normed, preferred_element_type=jnp.float32).astype(
        jnp.bfloat16
    )
    packed = packed.reshape(group_count, capacity, model_width)
    filled = jnp.any(slot_table, axis=2).reshape(slots_all)
    token_range = jnp.arange(rows_dev, dtype=jnp.int32)
    source_token = jnp.sum(
        slot_table.astype(jnp.int32) * token_range[None, None, :], axis=2
    ).reshape(slots_all)
    details = jnp.concatenate([expert_ids, gate_num], axis=1)[source_token]
    details = jnp.where(filled[:, None], details, -1).astype(jnp.bfloat16)
    details = details.reshape(group_count, capacity, 2 * top_count)
    arrived, arrived_details = (
        lax.all_to_all(packed, "grp", split_axis=0, concat_axis=0, tiled=True),
        lax.all_to_all(details, "grp", split_axis=0, concat_axis=0, tiled=True),
    )
    arrived = arrived.reshape(slots_all, model_width)
    arrived_details = arrived_details.reshape(slots_all, 2 * top_count).astype(jnp.int32)
    own_group = lax.axis_index("grp")
    own_half = lax.axis_index("loc") % 2
    is_lower = own_half == 0
    arrived_ids = arrived_details[:, :top_count]
    arrived_nums = arrived_details[:, top_count:]
    local_ids = arrived_ids - own_group * experts_group
    inside = (arrived_ids >= 0) & (local_ids >= 0) & (local_ids < experts_group)
    expert_range = jnp.arange(experts_group, dtype=jnp.int32)
    chosen = jnp.any(
        inside[:, :, None] & (local_ids[:, :, None] == expert_range[None, None, :]), axis=1
    )
    ranking = jnp.cumsum(chosen.astype(jnp.int32), axis=0) - 1
    slot_index = jnp.broadcast_to(jnp.arange(slots_all, dtype=jnp.int32)[:, None], chosen.shape)
    base_index = 2 * expert_range[None, :] * expert_rows + ranking
    spill_index = local_count * expert_rows
    target_lower = jnp.where(chosen, base_index, spill_index)
    target_upper = jnp.where(chosen, base_index + expert_rows, spill_index)
    source_slot = jnp.zeros((spill_index,), jnp.int32)
    source_slot = source_slot.at[target_lower.reshape(-1)].set(slot_index.reshape(-1), mode="drop")
    source_slot = source_slot.at[target_upper.reshape(-1)].set(slot_index.reshape(-1), mode="drop")
    outgoing = arrived[source_slot].reshape(local_count, expert_rows, model_width)
    received = lax.all_to_all(outgoing, "loc", split_axis=0, concat_axis=0, tiled=True)
    flat_rows = received.reshape(-1, model_width)
    gate_act = jnp.dot(flat_rows, w_gate[0], preferred_element_type=jnp.float32)
    up_act = jnp.dot(flat_rows, w_up[0], preferred_element_type=jnp.float32)
    hidden = (jax.nn.silu(gate_act) * up_act).astype(jnp.bfloat16)
    hidden = hidden.reshape(local_count, expert_rows, w_gate.shape[2])
    own_hidden = lax.dynamic_slice_in_dim(hidden, own_half * half_rows, half_rows, 1)
    given_hidden = lax.dynamic_slice_in_dim(hidden, (1 - own_half) * half_rows, half_rows, 1)
    taken_hidden, other_down = from_partner((given_hidden, w_down[0]), "loc", 0)
    hidden_full = ordered_pair(own_hidden, taken_hidden, is_lower, 2)
    down_full = ordered_pair(w_down[0], other_down, is_lower, 0)
    result = jnp.dot(
        hidden_full.reshape(-1, hidden_full.shape[2]), down_full, preferred_element_type=jnp.float32
    )
    result = result.astype(jnp.bfloat16).reshape(local_count, half_rows, model_width)
    returned = lax.all_to_all(result, "loc", split_axis=0, concat_axis=0, tiled=True)
    flat_returned = returned.reshape(-1, model_width)
    filled_slot = jnp.any(inside, axis=1)
    first_pick = jnp.argmax(inside, axis=1)
    second_pick = top_count - 1 - jnp.argmax(inside[:, ::-1], axis=1)

    def pick_term(which):
        local_pick = jnp.take_along_axis(local_ids, which[:, None], axis=1)[:, 0]
        local_pick = jnp.where(filled_slot, local_pick, 0)
        rank_pick = jnp.take_along_axis(ranking, local_pick[:, None], axis=1)[:, 0]
        row_pick = (2 * local_pick + rank_pick // half_rows) * half_rows + rank_pick % half_rows
        row_pick = jnp.where(filled_slot, row_pick, 0)
        weight = jnp.take_along_axis(arrived_nums, which[:, None], axis=1)[:, 0]
        weight = jnp.where(filled_slot, weight, 0).astype(jnp.float32) / denominator
        return weight[:, None] * flat_returned[row_pick].astype(jnp.float32)

    group_sum = (pick_term(first_pick) + pick_term(second_pick)).astype(jnp.bfloat16)
    group_sum = group_sum.reshape(group_count, capacity, model_width)
    returned_sums = lax.all_to_all(group_sum, "grp", split_axis=0, concat_axis=0, tiled=True)
    mixed_sum = jnp.dot(
        dispatch_matrix.T,
        returned_sums.reshape(slots_all, model_width),
        preferred_element_type=jnp.float32,
    )
    return (inputs_float + mixed_sum).astype(jnp.bfloat16)


MESH = pl.DeviceIdType.MESH
Z, X, Y, S, FA, FB, R1, R2A, R2B, R3X, R3Y, R4, D, RD = 0, 1, 2, 3, 7, 8, 9, 13, 14, 15, 16, 17, 18, 19
KINDS = 20


def flip(value, bit, unit):
    digit = (value // unit) % 2
    return value + unit * ((digit + bit) % 2 - digit)


def fused_kernel(
    tokens_ref, gain_ref, w_gate_ref, w_up_ref, w_down_ref, ids_ref, nums_ref, out_ref,
    rows, sums, from_sibling, diag_in, near_in, z_in, far_in, w_in, w_out, num_all,
    send_sem, recv_sem, z_send, w_sem, num_send, num_recv,
):
    grp, loc = lax.axis_index("grp"), lax.axis_index("loc")
    n_rows, width = tokens_ref.shape
    half = n_rows // 2
    hidden_units = w_gate_ref.shape[2]
    experts = num_all.shape[1]
    sibling = (flip(grp, 1, 1), loc)
    along_x = (flip(grp, 1, 2), loc)
    along_y = (flip(grp, 1, 4), loc)
    me = grp * 4 + loc
    everyone = 32
    upper = loc // 2
    mirrored = loc + upper * (3 - 2 * loc)
    outer, inner, far_inner = 3 * upper, 1 + upper, 2 - upper

    def plane(i):
        from_end = (i // 2) * i + (1 - i // 2) * ((mirrored + i) % 2)
        return from_end + upper * (3 - 2 * from_end)

    def worked(k):
        return plane((k + 1) % 4)

    barrier = pltpu.get_barrier_semaphore()

    @pl.loop(1, everyone)
    def _(i):
        other = (me + i) % everyone
        pl.semaphore_signal(barrier, 1, device_id=(other // 4, other % 4), device_id_type=MESH)

    weight_copies = (
        pltpu.make_async_copy(w_gate_ref.at[0], w_in.at[:, pl.ds(0, hidden_units)], w_sem.at[0]),
        pltpu.make_async_copy(
            w_up_ref.at[0], w_in.at[:, pl.ds(hidden_units, hidden_units)], w_sem.at[1]
        ),
        pltpu.make_async_copy(w_down_ref.at[0], w_out, w_sem.at[2]),
    )
    inputs = tokens_ref[...].astype(jnp.float32)
    inv_scale = lax.rsqrt(jnp.mean(inputs * inputs, axis=-1, keepdims=True) + epsilon)
    rows[4 * loc, pl.ds(0, n_rows), :] = (
        inputs * inv_scale * gain_ref[...].astype(jnp.float32)[None, :]
    ).astype(jnp.bfloat16)
    pl.semaphore_wait(barrier, everyone - 1)

    def remote(kind, j, source, target, device):
        return pltpu.make_async_remote_copy(
            src_ref=source,
            dst_ref=target,
            send_sem=send_sem.at[kind * 4 + j],
            recv_sem=recv_sem.at[kind * 4 + j],
            device_id=device,
            device_id_type=MESH,
        )

    own, other_core = pl.ds(0, n_rows), pl.ds(n_rows, n_rows)
    first, second = pl.ds(0, half), pl.ds(half, half)

    def copy_z(j, index, target):
        return pltpu.make_async_remote_copy(
            src_ref=rows.at[4 * j, own],
            dst_ref=rows.at[4 * j, own],
            send_sem=z_send.at[index],
            recv_sem=recv_sem.at[Z * 4 + j],
            device_id=(grp, target),
            device_id_type=MESH,
        )

    def copy_d(j, index, target):
        return pltpu.make_async_remote_copy(
            src_ref=rows.at[4 * j + 3, own],
            dst_ref=rows.at[4 * j + 3, own],
            send_sem=z_send.at[5 + index],
            recv_sem=recv_sem.at[D * 4 + j],
            device_id=(grp, target),
            device_id_type=MESH,
        )

    def copy_rd(j):
        return pltpu.make_async_remote_copy(
            src_ref=sums.at[4 * j + 3],
            dst_ref=far_in.at[loc],
            send_sem=send_sem.at[RD * 4 + j],
            recv_sem=recv_sem.at[RD * 4 + loc],
            device_id=(grp, j),
            device_id_type=MESH,
        )

    def add_far(j):
        pltpu.make_async_remote_copy(
            src_ref=far_in.at[j],
            dst_ref=far_in.at[j],
            send_sem=send_sem.at[RD * 4 + j],
            recv_sem=recv_sem.at[RD * 4 + j],
            device_id=(grp, j),
            device_id_type=MESH,
        ).wait_recv()
        t = 4 * loc + 3
        total = sums[t].astype(jnp.float32) + far_in[j].astype(jnp.float32)
        sums[t] = total.astype(jnp.bfloat16)

    def copy_x(j):
        return remote(X, j, rows.at[4 * j, own], rows.at[4 * j + 1, own], along_x)

    def copy_y(j):
        return remote(Y, j, rows.at[4 * j, own], rows.at[4 * j + 2, own], along_y)

    def copy_s(j, q):
        t = 4 * j + q
        return remote(S + q, j, rows.at[t, own], rows.at[t, other_core], sibling)

    def copy_fa(j):
        return remote(FA, j, rows.at[4 * j + 1, first], rows.at[4 * j + 3, first], along_y)

    def copy_fb(j):
        return remote(FB, j, rows.at[4 * j + 2, second], rows.at[4 * j + 3, second], along_x)

    def copy_r1(j, q):
        t = 4 * j + q
        return remote(R1 + q, j, rows.at[t, other_core], from_sibling.at[t], sibling)

    def copy_r2a(j):
        return remote(R2A, j, sums.at[4 * j + 3, first], diag_in.at[j, first], along_x)

    def copy_r2b(j):
        return remote(R2B, j, sums.at[4 * j + 3, second], diag_in.at[j, second], along_y)

    def copy_r3x(j):
        return remote(R3X, j, sums.at[4 * j + 1], near_in.at[j, 0], along_x)

    def copy_r3y(j):
        return remote(R3Y, j, sums.at[4 * j + 2], near_in.at[j, 1], along_y)

    def copy_r4(j):
        return pltpu.make_async_remote_copy(
            src_ref=sums.at[4 * j],
            dst_ref=z_in.at[loc],
            send_sem=send_sem.at[R4 * 4 + j],
            recv_sem=recv_sem.at[R4 * 4 + loc],
            device_id=(grp, j),
            device_id_type=MESH,
        )

    def arrival_r4(j):
        return pltpu.make_async_remote_copy(
            src_ref=z_in.at[j],
            dst_ref=z_in.at[j],
            send_sem=send_sem.at[R4 * 4 + j],
            recv_sem=recv_sem.at[R4 * 4 + j],
            device_id=(grp, j),
            device_id_type=MESH,
        )

    def numerator_copy(source, target, device):
        return pltpu.make_async_remote_copy(
            src_ref=source,
            dst_ref=target,
            send_sem=num_send,
            recv_sem=num_recv,
            device_id=device,
            device_id_type=MESH,
        )

    def spread(j):
        copy_x(j).start()
        copy_y(j).start()
        copy_s(j, 0).start()

    def forward(j, diagonal):
        copy_x(j).wait_recv()
        if diagonal:
            copy_fa(j).start()
        copy_s(j, 1).start()
        copy_y(j).wait_recv()
        if diagonal:
            copy_fb(j).start()
        copy_s(j, 2).start()

    def take_diagonal(i):
        copy_d(plane(i), 2, outer).wait_recv()
        copy_s(plane(i), 3).start()

    def forward_diagonal(j):
        copy_fa(j).wait_recv()
        copy_fb(j).wait_recv()
        copy_s(j, 3).start()

    def add(t, extra=(), place=None):
        place = pl.ds(0, n_rows) if place is None else place
        total = sums[t, place, :].astype(jnp.float32)
        total += from_sibling[t, place, :].astype(jnp.float32)
        for term in extra:
            total += term[place, :].astype(jnp.float32)
        sums[t, place, :] = total.astype(jnp.bfloat16)

    def reduce_diagonal(j):
        copy_r2a(j).start()
        copy_r2b(j).start()

    def add_sibling(j):
        copy_r1(j, 3).wait_recv()
        add(4 * j + 3)

    def reduce_near(j):
        copy_r1(j, 1).wait_recv()
        add(4 * j + 1, (), first)
        copy_r2b(j).wait_recv()
        add(4 * j + 1, (diag_in.at[j],), second)
        copy_r3x(j).start()
        copy_r1(j, 2).wait_recv()
        add(4 * j + 2, (), second)
        copy_r2a(j).wait_recv()
        add(4 * j + 2, (diag_in.at[j],), first)
        copy_r3y(j).start()

    def reduce_near_only(j):
        copy_r1(j, 1).wait_recv()
        add(4 * j + 1)
        copy_r3x(j).start()
        copy_r1(j, 2).wait_recv()
        add(4 * j + 2)
        copy_r3y(j).start()

    def reduce_plane(j):
        copy_r1(j, 0).wait_recv()
        copy_r3x(j).wait_recv()
        copy_r3y(j).wait_recv()
        add(4 * j, (near_in.at[j, 0], near_in.at[j, 1]))

    is_inner = mirrored == 1

    def take_plane(i, target):
        copy_z(plane(i), 1 + i, target).wait_recv()

        @pl.when(is_inner)
        def _():
            copy_z(plane(i), 1 + i, target).start()

        spread(plane(i))

    @pl.when(is_inner)
    def _():
        copy_z(loc, 0, outer).start()
        copy_z(loc, 1, far_inner).start()

    @pl.when(mirrored == 0)
    def _():
        copy_z(loc, 0, inner).start()

    spread(loc)
    for copy in weight_copies:
        copy.start()
    expert_row = lax.broadcasted_iota(jnp.int32, (experts, n_rows), 0)
    numerators = jnp.zeros((experts, n_rows), jnp.int32)
    for k in range(ids_ref.shape[0]):
        numerators += jnp.where(ids_ref[k : k + 1, :] == expert_row, nums_ref[k : k + 1, :], 0)
    num_all[me] = numerators.astype(jnp.float32).astype(jnp.bfloat16)

    @pl.loop(1, everyone)
    def _(i):
        other = (me + i) % everyone
        numerator_copy(num_all.at[me], num_all.at[me], (other // 4, other % 4)).start()

    forward(loc, True)
    take_plane(1, far_inner)
    take_plane(2, outer)
    forward_diagonal(loc)

    @pl.when(is_inner)
    def _():
        copy_d(loc, 0, outer).start()
        copy_d(loc, 1, far_inner).start()

    @pl.when(mirrored == 0)
    def _():
        copy_d(loc, 0, inner).start()

    forward(plane(1), False)
    take_plane(3, outer)
    numerator_copy(
        num_all.at[pl.ds(0, everyone - 1)], num_all.at[pl.ds(0, everyone - 1)], sibling
    ).wait_recv()

    for copy in weight_copies:
        copy.wait()
    own_expert = grp * 2 + loc // 2
    pick = (expert_row == own_expert).astype(jnp.float32).astype(jnp.bfloat16)

    def weights_of(j, q, core_flip):
        source = flip(flip(flip(grp, core_flip, 1), q % 2, 2), q // 2, 4)
        place = source * 4 + j
        return lax.dot_general(
            num_all[place], pick, (((0,), (0,)), ((), ())), preferred_element_type=jnp.float32
        )[:, :1] * (1.0 / denominator)

    @pl.loop(0, 16)
    def _(step):
        k, q = step // 4, step % 4
        j = worked(k)
        t = 4 * j + q

        @pl.when(q == 0)
        def _():
            @pl.when(k >= 2)
            def _():
                reduce_plane(worked(k - 2))
                copy_r4(worked(k - 2)).start()

            copy_s(j, 0).wait_recv()

        @pl.when(q == 1)
        def _():
            @pl.when(k >= 1)
            def _():
                add_sibling(worked(k - 1))

                @pl.when(k < 3)
                def _():
                    copy_rd(worked(k - 1)).start()

                @pl.when(k == 3)
                def _():
                    reduce_diagonal(worked(k - 1))

            @pl.when(k == 0)
            def _():
                take_diagonal(1)

                @pl.when(is_inner)
                def _():
                    take_diagonal(2)
                    copy_d(plane(2), 2, outer).start()

            @pl.when((k == 1) & (mirrored == 0))
            def _():
                take_diagonal(2)

            @pl.when(k == 2)
            def _():
                forward_diagonal(j)

            copy_s(j, 1).wait_recv()

        @pl.when(q == 2)
        def _():
            @pl.when((k >= 1) & (k < 3))
            def _():
                reduce_near_only(worked(k - 1))

            @pl.when(k == 3)
            def _():
                reduce_near(worked(k - 1))

            copy_s(j, 2).wait_recv()

        @pl.when(q == 3)
        def _():
            @pl.when(k == 0)
            def _():
                forward(plane(2), False)

            @pl.when(k == 1)
            def _():
                forward(plane(3), True)

            copy_s(j, 3).wait_recv()

        both = jnp.dot(rows[t], w_in[...], preferred_element_type=jnp.float32)
        gate_act, up_act = both[:, :hidden_units], both[:, hidden_units:]
        hidden = (jax.nn.silu(gate_act) * up_act).astype(jnp.bfloat16)
        weight = jnp.concatenate([weights_of(j, q, 0), weights_of(j, q, 1)], axis=0)
        piece = width // 4
        for part in range(4):
            columns = pl.ds(part * piece, piece)
            result = jnp.dot(
                hidden, w_out[:, columns], preferred_element_type=jnp.float32
            )
            result = (result * weight).astype(jnp.bfloat16)
            sums[t, :, columns] = result[:n_rows]
            rows[t, other_core, columns] = result[n_rows:]
        for which in range(4):
            @pl.when(q == which)
            def _():
                copy_r1(j, which).start()

    add_sibling(loc)

    @pl.when(is_inner)
    def _():
        for i in (1, 2, 3):
            add_far(plane(i))

    @pl.when(mirrored == 0)
    def _():
        add_far(plane(1))

    reduce_diagonal(loc)
    reduce_plane(worked(2))
    copy_r4(worked(2)).start()
    reduce_near(loc)
    reduce_plane(loc)
    total = tokens_ref[...].astype(jnp.float32) + sums[4 * loc].astype(jnp.float32)
    for i in (1, 2, 3):
        arrival_r4(plane(i)).wait_recv()
        total += z_in[plane(i)].astype(jnp.float32)
    out_ref[...] = total.astype(jnp.bfloat16)

    copy_z(loc, 0, outer).wait_send()
    copy_d(loc, 0, outer).wait_send()
    for i in (1, 2):
        copy_rd(plane(i)).wait_send()
    for j in (loc, plane(3)):
        for make in (copy_fa, copy_fb, copy_r2a, copy_r2b):
            make(j).wait_send()

    @pl.when(is_inner)
    def _():
        copy_z(loc, 1, far_inner).wait_send()
        copy_d(loc, 1, far_inner).wait_send()
        copy_d(plane(2), 2, outer).wait_send()
        for i in (1, 2, 3):
            copy_z(plane(i), 1 + i, outer).wait_send()

    for i in (1, 2, 3):
        copy_r4(plane(i)).wait_send()

    @pl.loop(0, 4)
    def _(j):
        copy_x(j).wait_send()
        copy_y(j).wait_send()
        for q in range(4):
            copy_s(j, q).wait_send()
            copy_r1(j, q).wait_send()
        copy_r3x(j).wait_send()
        copy_r3y(j).wait_send()

    numerator_copy(
        num_all.at[pl.ds(0, everyone - 1)], num_all.at[pl.ds(0, everyone - 1)], sibling
    ).wait_send()


def fused(tokens, norm_gain, w_gate, w_up, w_down, expert_ids, gate_num):
    n_rows, width = tokens.shape
    hidden_units = w_gate.shape[2]
    bf16 = jnp.bfloat16
    return pl.pallas_call(
        fused_kernel,
        out_shape=jax.ShapeDtypeStruct(tokens.shape, tokens.dtype),
        in_specs=[
            pl.BlockSpec(memory_space=pl.ANY if 2 <= operand < 5 else pltpu.VMEM)
            for operand in range(7)
        ],
        out_specs=pl.BlockSpec(memory_space=pltpu.VMEM),
        scratch_shapes=[
            pltpu.VMEM((16, 2 * n_rows, width), bf16),
            pltpu.VMEM((16, n_rows, width), bf16),
            pltpu.VMEM((16, n_rows, width), bf16),
            pltpu.VMEM((4, n_rows, width), bf16),
            pltpu.VMEM((4, 2, n_rows, width), bf16),
            pltpu.VMEM((4, n_rows, width), bf16),
            pltpu.VMEM((4, n_rows, width), bf16),
            pltpu.VMEM((width, 2 * hidden_units), bf16),
            pltpu.VMEM((hidden_units, width), bf16),
            pltpu.VMEM((32, 16, n_rows), bf16),
            pltpu.SemaphoreType.DMA((KINDS * 4,)),
            pltpu.SemaphoreType.DMA((KINDS * 4,)),
            pltpu.SemaphoreType.DMA((8,)),
            pltpu.SemaphoreType.DMA((3,)),
            pltpu.SemaphoreType.DMA,
            pltpu.SemaphoreType.DMA,
        ],
        compiler_params=pltpu.CompilerParams(
            collective_id=0, has_side_effects=True, vmem_limit_bytes=60 * 2**20
        ),
        cost_estimate=pl.CostEstimate(
            flops=2 * 32 * n_rows * width * hidden_units * 3,
            bytes_accessed=2 * width * hidden_units * 3,
            transcendentals=32 * n_rows * hidden_units,
        ),
    )(tokens, norm_gain, w_gate, w_up, w_down, expert_ids.T, gate_num.T)


def shards(tokens, *others):
    if (lax.axis_size("grp"), lax.axis_size("loc")) == (8, 4):
        return fused(tokens, *others)
    return routed(tokens, *others)


def solution(mesh):
    return jax.shard_map(
        shards,
        mesh=mesh,
        in_specs=(
            P(("grp", "loc"), None),
            P(),
            P(("grp", "loc"), None, None),
            P(("grp", "loc"), None, None),
            P(("grp", "loc"), None, None),
            P(("grp", "loc"), None),
            P(("grp", "loc"), None),
        ),
        out_specs=P(("grp", "loc"), None),
        check_vma=False,
    )
```
